256 devices in a mesh: dp: 32 (over y_lo, z, core), code: 8 (over x, y_hi).
Axes of the slice: x: 4, y: 4 (y_hi: 2, y_lo: 2; y = y_hi * 2 + y_lo), z: 8, core: 2. Of those that a mesh axis runs over, the one named last changes fastest.
Arguments:
- latents: bfloat16 [8192, 256], P('dp'), may hold values from -128 to 128
- grads: bfloat16 [8192, 256], P('dp'), may hold values from -6 to 6
- codebook: bfloat16 [131072, 256], P(('dp', 'code')), may hold values from -2 to 2
- hard_code: int32 [8192], P('dp'), may hold values from 0 to 131071
Outputs:
- grad_latents: float32 [8192, 256], P('dp')
- grad_codebook: float32 [131072, 256], P(('dp', 'code'))
The draws below stay inside these ranges and needn't reach their ends.
All inputs are finite; a program needn't handle non-finite values.
Results may differ from the reference program's by a relative error of at most 0.0034.
Values may be sent and summed in bfloat16 or wider, within the bound.
A program may use at most 192 MiB of HBM per device.

```python
import math
import jax
import jax.numpy as jnp
from jax import lax

D = 256
VOCAB = 131072
TOKENS = 8192
N_DP = 32
N_CODE = 8


def code_table(key):
    key = jax.random.fold_in(key, 11)
    first_key, second_key = jax.random.split(key)
    base = jax.random.normal(first_key, (VOCAB, D), jnp.float32)
    rows = jnp.arange(VOCAB)
    owner = rows // (VOCAB // (N_DP * N_CODE))
    along_code = (owner % N_CODE).astype(jnp.float32) / max(N_CODE - 1, 1)
    along_data = (owner // N_CODE).astype(jnp.float32) / max(N_DP - 1, 1)
    spread = jnp.exp(jax.random.uniform(second_key, (VOCAB,), jnp.float32, -0.1, 0.1))
    scale = 2.5 * (1.0 + 0.4 * along_code) * (1.0 + 0.05 * along_data) * spread / D ** 0.5
    return jnp.clip(base * scale[:, None], -2.0, 2.0)


def draw_codebook(key, part):
    return code_table(key).astype(jnp.bfloat16)


def draw_latents(key, part):
    key = jax.random.fold_in(key, 23)
    keys = jax.random.split(key, 8)
    member = jax.random.randint(keys[6], (TOKENS,), 0, 8)
    centres = jax.random.normal(keys[7], (8, D), jnp.float32)
    noise = jax.random.normal(keys[0], (TOKENS, D), jnp.float32)
    row_scale = jnp.exp(jax.random.uniform(keys[1], (TOKENS, 1), jnp.float32, -0.25, 0.25))
    latent = 0.62 * row_scale * (0.86 * centres[member] + 0.5 * noise)
    return latent.astype(jnp.bfloat16)


def draw_grads(key, part):
    key = jax.random.fold_in(key, 37)
    keys = jax.random.split(key, 2)
    shared = jax.random.normal(keys[0], (1, D), jnp.float32)
    noise = jax.random.normal(keys[1], (TOKENS, D), jnp.float32)
    values = 0.75 * shared + 0.66 * noise
    return jnp.clip(values, -6.0, 6.0).astype(jnp.bfloat16)


def set_ends(entries, stream_key, least, largest):
    longest = entries.shape.index(max(entries.shape))
    spots = []
    for shift in (0, 1):
        where = [jax.random.randint(jax.random.fold_in(stream_key, axis), (), 0, length) for axis, length in enumerate(entries.shape)]
        where[longest] = (where[longest] + shift) % entries.shape[longest]
        spots.append(tuple(where))
    return entries.at[spots[0]].set(least).at[spots[1]].set(largest)


def setup_inputs(seed: int = 0) -> dict:
    key_list = jax.random.split(jax.random.key(seed), 5)
    return {
        "latents": draw_latents(jax.random.fold_in(key_list[4], 71), 0),
        "grads": draw_grads(jax.random.fold_in(key_list[4], 71), 0),
        "codebook": draw_codebook(jax.random.fold_in(key_list[4], 71), 0),
        "hard_code": set_ends(jax.random.randint(key_list[3], (TOKENS,), 0, VOCAB), jax.random.fold_in(key_list[3], 1), 0, VOCAB - 1).astype(jnp.int32),
    }


def reference(latents, grads, codebook, hard_code):
    tokens = latents.shape[0]
    width = math.gcd(VOCAB, 4096)
    blocks = VOCAB // width
    stacked = jnp.concatenate([latents, grads], axis=0)
    table = codebook.reshape(blocks, width, D)

    def first(carry, block):
        top_old, total_old, weighted_old = carry
        both = jnp.dot(stacked, block.T, preferred_element_type=jnp.float32)
        logit = both[:tokens]
        pull = both[tokens:]
        top = jnp.maximum(top_old, jnp.max(logit, axis=1))
        expo = jnp.exp(logit - top[:, None])
        factor = jnp.exp(top_old - top)
        return (top, total_old * factor + jnp.sum(expo, axis=1), weighted_old * factor + jnp.sum(expo * pull, axis=1)), None

    start = (jnp.full((tokens,), -1e30, jnp.float32), jnp.zeros((tokens,), jnp.float32), jnp.zeros((tokens,), jnp.float32))
    (top, total, weighted), unused = lax.scan(first, start, table)
    mean_pull = weighted / total

    def second(acc, block):
        both = jnp.dot(stacked, block.T, preferred_element_type=jnp.float32)
        logit = both[:tokens]
        pull = both[tokens:]
        probs = jnp.exp(logit - top[:, None]) / total[:, None]
        dlogits = (probs * (pull - mean_pull[:, None])).astype(jnp.bfloat16)
        acc = acc + jnp.dot(dlogits, block, preferred_element_type=jnp.float32)
        part = jnp.dot(dlogits.T, latents, preferred_element_type=jnp.float32)
        return acc, part

    grad_latents, parts = lax.scan(second, jnp.zeros((tokens, D), jnp.float32), table)
    hard_rows = jnp.zeros((VOCAB, D), jnp.float32).at[hard_code].add(grads.astype(jnp.float32))
    grad_codebook = parts.reshape(VOCAB, D) + hard_rows
    return grad_latents, grad_codebook
```

```python
import functools

import jax
import jax.numpy as jnp
from jax import lax
from jax.experimental import pallas as pl
from jax.experimental.pallas import tpu as pltpu
from jax.sharding import PartitionSpec as P

MESH = pl.DeviceIdType.MESH
F32 = jnp.float32
BF16 = jnp.bfloat16

NX, NY, NZ, NC = 4, 4, 8, 2

S_X = 0
S_P = 4
S_M = 9
S_YA = 14
S_YB = 19
S_C = 24
S_ST1 = 44
S_ST2 = 52
S_ST3 = 60
S_GC = 68
S_GY = 72
S_GZ = 76
S_AG = 84
S_GX = 92
S_ALL = 96


def device(x, y, z, c):
    return ((y % 2 * NZ + z) * NC + c, x * 2 + y // 2)


def nt_dot(a, b):
    return lax.dot_general(a, b, (((1,), (1,)), ((), ())), preferred_element_type=F32)


def kernel(
    lat, gr, cb, hc, olat, ocb,
    LAT, GR, HC, CB, CBT, E, PU, D, MB, ST, ST1, ST2, FIN,
    GCT, GCR, GYK, GYT, GYR, GZK, GZT, GZR, GA, GXT, GXR,
    ss, rs,
):
    T = lat.shape[0]
    K = cb.shape[0]
    half = T // 2
    part = T // NZ
    dp = lax.axis_index("dp")
    code = lax.axis_index("code")
    c = dp % NC
    z = dp // NC % NZ
    yl = dp // (NC * NZ)
    x = code // 2
    yh = code % 2
    y = yh * 2 + yl
    a = (z - x + NZ) % NZ

    def at(dx=0, dy=0, dz=0, dc=0):
        return device((x + dx) % NX, (y + dy) % NY, (z + dz) % NZ, (c + dc) % NC)

    def copy(src, dst, dev, i, j=None):
        return pltpu.make_async_remote_copy(
            src_ref=src, dst_ref=dst, send_sem=ss.at[i], recv_sem=rs.at[i if j is None else j],
            device_id=dev, device_id_type=MESH,
        )

    def send(src, dst, dev, i, j=None):
        copy(src, dst, dev, i, j).start()

    def recv(dst, i):
        copy(dst, dst, at(dc=1), i).wait_recv()

    def sent(src, i):
        copy(src, src, at(dc=1), i).wait_send()

    yc = [(dy, dc) for dc in range(NC) for dy in range(NY) if dy or dc]

    barrier = pltpu.get_barrier_semaphore()

    def greet(dev):
        pl.semaphore_signal(barrier, inc=1, device_id=dev, device_id_type=MESH)

    for d in range(1, NX):
        greet(at(dx=d))
    for dy, dc in yc:
        greet(at(dy=dy, dc=dc))
    for d in range(1, NZ):
        greet(at(dz=d))
    home = z == x + NX * yh
    for zs in range(NZ):
        @pl.when(jnp.logical_not(home & (z == zs)))
        def _(zs=zs):
            greet(device(z % NX, z // NX * 2 + yl, zs, c))

    peers = NX - 1 + len(yc) + NZ - 1 + 8
    pl.semaphore_wait(barrier, jnp.where(home, peers - 1, peers))

    send(cb, CB.at[x], at(dx=1), S_X)
    send(cb, CB.at[x], at(dx=NX - 1), S_X + 1)

    def chunk(c_, yl_, b_):
        return (c_ * 2 + yl_) * 2 + b_

    def pieces(q):
        for arr in (LAT, GR):
            for h in range(2):
                yield arr.at[pl.ds(pl.multiple_of(q * T + h * half, half), half)]
        yield HC.at[q]

    b_own = a // NX
    q_own = chunk(c, yl, b_own)
    b_sp = a // NX
    b_rp = (a + NZ - 1) % NZ // NX
    b_sm = (NZ - a) % NZ // NX
    b_rm = (2 * NZ - 1 - a) % NZ // NX
    source = a % NX == 0
    last = a % NX == 1

    @pl.when(source)
    def _():
        rows = pl.ds(pl.multiple_of(q_own * T, T), T)
        LAT[rows, :] = lat[...]
        GR[rows, :] = gr[...]
        HC[q_own] = hc[...]
        for p, piece in enumerate(pieces(q_own)):
            send(piece, piece, at(dz=1), S_P + p)
            send(piece, piece, at(dz=NZ - 1), S_M + p)

    CB[x] = cb[...]

    sp = list(pieces(chunk(c, yl, b_sp)))
    sm = list(pieces(chunk(c, yl, b_sm)))
    rp = list(pieces(chunk(c, yl, b_rp)))
    rm = list(pieces(chunk(c, yl, b_rm)))
    pa = list(pieces(chunk(c, yl, 0)))
    pb = list(pieces(chunk(c, yl, 1)))
    oa = list(pieces(chunk(c, 1 - yl, 0)))
    ob = list(pieces(chunk(c, 1 - yl, 1)))
    for p in range(5):
        recv(rp[p], S_P + p)

        @pl.when(jnp.logical_not(source))
        def _(p=p):
            send(rp[p], rp[p], at(dz=1), S_P + p)
            recv(rm[p], S_M + p)

            @pl.when(jnp.logical_not(last))
            def _():
                send(rm[p], rm[p], at(dz=NZ - 1), S_M + p)

        send(pa[p], pa[p], at(dy=1), S_YA + p)
        send(pb[p], pb[p], at(dy=NY - 1), S_YB + p)
        send(pa[p], pa[p], at(dc=1), S_C + p)
        send(pb[p], pb[p], at(dc=1), S_C + 5 + p)
        if p == 2:
            left = (x + NX - 1) % NX
            right = (x + 1) % NX
            far = (x + 2) % NX
            recv(CB.at[left], S_X)
            send(CB.at[left, pl.ds(0, K // 2)], CB.at[left, pl.ds(0, K // 2)], at(dx=1), S_X + 2)
            recv(CB.at[right], S_X + 1)
            send(CB.at[right, pl.ds(K // 2, K // 2)], CB.at[right, pl.ds(K // 2, K // 2)], at(dx=NX - 1), S_X + 3)
    for p in range(5):
        recv(oa[p], S_YA + p)
        send(oa[p], oa[p], at(dc=1), S_C + 10 + p)
        recv(ob[p], S_YB + p)
        send(ob[p], ob[p], at(dc=1), S_C + 15 + p)
    recv(CB.at[far, pl.ds(0, K // 2)], S_X + 2)
    recv(CB.at[far, pl.ds(K // 2, K // 2)], S_X + 3)
    other = [
        list(pieces(chunk(1 - c, yl_, b_)))
        for yl_, b_ in ((yl, 0), (yl, 1), (1 - yl, 0), (1 - yl, 1))
    ]
    for k in range(4):
        for p in range(5):
            recv(other[k][p], S_C + 5 * k + p)

    for j in range(NX):
        CBT[:, j * K:(j + 1) * K] = CB[j].T

    def first(q, carry):
        rows = pl.ds(pl.multiple_of(q * T, T), T)

        def inner(j, stats):
            top_old, total_old, weighted_old = stats
            codes = CB[j]
            logit = nt_dot(codes, LAT[rows, :])
            pull = nt_dot(codes, GR[rows, :])
            top = jnp.max(logit, axis=0, keepdims=True)
            expo = jnp.exp(logit - top)
            E[q, j] = expo
            PU[q, j] = pull
            MB[q, j] = jnp.broadcast_to(top, (8, T))
            total = jnp.sum(expo, axis=0, keepdims=True)
            weighted = jnp.sum(expo * pull, axis=0, keepdims=True)
            return merge((top_old, total_old, weighted_old), (top, total, weighted))

        start = (jnp.full((1, T), -1e30, F32), jnp.zeros((1, T), F32), jnp.zeros((1, T), F32))
        top, total, weighted = lax.fori_loop(0, NX, inner, start)
        ST[q] = jnp.concatenate([top, total, weighted, jnp.zeros((5, T), F32)], axis=0)
        return carry

    def merge(one, two):
        top = jnp.maximum(one[0], two[0])
        low = jnp.exp(one[0] - top)
        high = jnp.exp(two[0] - top)
        return (top, one[1] * low + two[1] * high, one[2] * low + two[2] * high)

    def merge_all(terms):
        total = None
        for t in terms:
            rows = (t[0:1], t[1:2], t[2:3])
            total = rows if total is None else merge(total, rows)
        return total

    def pack(rows):
        return jnp.concatenate([*rows, jnp.zeros((5, T), F32)], axis=0)

    lax.fori_loop(0, 8, first, 0)

    def mine(y_, c_):
        return chunk(c_, y_ % 2, y_ // 2)

    q_me = mine(y, c)
    for dy, dc in yc:
        n = dc * NY + dy
        send(ST.at[mine((y + dy) % NY, (c + dc) % NC)], ST1.at[n], at(dy=dy, dc=dc), S_ST1 + n)
    for dy, dc in yc:
        recv(ST1.at[dc * NY + dy], S_ST1 + dc * NY + dy)
    ST2[0] = pack(merge_all([ST[q_me]] + [ST1[dc * NY + dy] for dy, dc in yc]))
    for d in range(1, NZ):
        send(ST2.at[0], ST2.at[d], at(dz=d), S_ST2 + d)
    for d in range(1, NZ):
        recv(ST2.at[d], S_ST2 + d)
    top, total, weighted = merge_all([ST2[d] for d in range(NZ)])
    FIN[q_me] = pack((top, 1.0 / total, weighted / total))
    for dy, dc in yc:
        n = dc * NY + dy
        send(FIN.at[q_me], FIN.at[q_me], at(dy=dy, dc=dc), S_ST3 + n)
    for dy, dc in yc:
        recv(FIN.at[mine((y + NY - dy) % NY, (c + dc) % NC)], S_ST3 + dc * NY + dy)

    def latent_grad(q):
        fin = FIN[q]
        cols = pl.ds(pl.multiple_of(q * T, T), T)

        def inner(j, carry):
            factor = jnp.exp(MB[q, j][0:1] - fin[0:1]) * fin[1:2]
            dlog = (E[q, j] * factor) * (PU[q, j] - fin[2:3])
            D[pl.ds(pl.multiple_of(j * K, K), K), cols] = dlog.astype(BF16)
            return carry

        lax.fori_loop(0, NX, inner, 0)
        return jnp.dot(CBT[...], D[:, cols], preferred_element_type=F32).T

    def for_other(k, carry):
        GCT[k] = latent_grad((1 - c) * 4 + k)
        send(GCT.at[k], GCR.at[k], at(dc=1), S_GC + k)
        return carry

    lax.fori_loop(0, 4, for_other, 0)

    def for_own(d, carry):
        y_ = (y + d) % NY
        k = y_ % 2 * 2 + y_ // 2
        total = latent_grad(c * 4 + k)
        recv(GCR.at[k], S_GC + k)
        total = total + GCR[k]

        @pl.when(d == 0)
        def _():
            GYK[...] = total

        @pl.when(d > 0)
        def _():
            GYT[d] = total.astype(BF16)
            send(GYT.at[d], GYR.at[d], at(dy=d), S_GY + d)

        return carry

    lax.fori_loop(0, 4, for_own, 0)

    base = ((yl * NZ + z) * NC + c) * 8 + yh

    def codebook_grad(d):
        j = (x + d) % NX
        first_code = (base + j * 2) * K
        acc = jnp.dot(D[pl.ds(pl.multiple_of(j * K, K), K), :], LAT[...], preferred_element_type=F32)
        ids = first_code + lax.broadcasted_iota(jnp.int32, (K, T), 0)
        for q in range(8):
            hit = jnp.where(HC[q][0:1] == ids, 1.0, 0.0).astype(BF16)
            acc = acc + jnp.dot(hit, GR[q * T:(q + 1) * T, :], preferred_element_type=F32)
        return acc

    def codebook_send(d):
        GXT[d] = codebook_grad(d).astype(BF16)
        send(GXT.at[d], GXR.at[d], at(dx=d), S_GX + d)

    codebook_send(2)

    total = GYK[...]
    for d in range(1, NY):
        recv(GYR.at[d], S_GY + d)
        total = total + GYR[d].astype(F32)
    GZK[...] = total
    GZT[...] = total.astype(BF16)
    for d in range(1, NZ):
        rows = pl.ds(pl.multiple_of((z + d) % NZ * part, part), part)
        send(GZT.at[rows], GZR.at[d], at(dz=d), S_GZ + d)

    codebook_send(1)
    codebook_send(3)

    total = GZK[pl.ds(pl.multiple_of(z * part, part), part), :]
    for d in range(1, NZ):
        recv(GZR.at[d], S_GZ + d)
        total = total + GZR[d].astype(F32)
    GA[...] = total
    dst = olat.at[pl.ds(pl.multiple_of(z * part, part), part)]
    for dx in range(NX):
        for dh in range(2):
            dev = device((x + dx) % NX, (yh + dh) % 2 * 2 + yl, x + NX * yh, c)
            if dx or dh:
                send(GA, dst, dev, S_AG + dx * 2 + dh, S_AG + z)
            else:
                @pl.when(jnp.logical_not(home))
                def _(dev=dev):
                    send(GA, dst, dev, S_AG, S_AG + z)

                @pl.when(home)
                def _():
                    olat[pl.ds(pl.multiple_of(z * part, part), part), :] = GA[...]

    total = codebook_grad(0)
    for d in range(1, NX):
        recv(GXR.at[d], S_GX + d)
        total = total + GXR[d].astype(F32)
    ocb[...] = total

    for zs in range(NZ):
        @pl.when(jnp.logical_not(home & (z == zs)))
        def _(zs=zs):
            recv(olat.at[pl.ds(zs * part, part)], S_AG + zs)

    sent(cb, S_X)
    sent(cb, S_X + 1)
    sent(CB.at[0, pl.ds(0, K // 2)], S_X + 2)
    sent(CB.at[0, pl.ds(0, K // 2)], S_X + 3)
    for p in range(5):
        sent(sp[p], S_P + p)

        @pl.when(jnp.logical_not(last))
        def _(p=p):
            sent(sm[p], S_M + p)

        sent(pa[p], S_YA + p)
        sent(pb[p], S_YB + p)
        for k, own in enumerate((pa, pb, oa, ob)):
            sent(own[p], S_C + 5 * k + p)
    for dy, dc in yc:
        n = dc * NY + dy
        sent(ST.at[0], S_ST1 + n)
        sent(FIN.at[0], S_ST3 + n)
    for d in range(1, NZ):
        sent(ST2.at[0], S_ST2 + d)
        sent(GZT.at[pl.ds(0, part)], S_GZ + d)
    for k in range(4):
        sent(GCT.at[k], S_GC + k)
    for d in range(1, NY):
        sent(GYT.at[d], S_GY + d)
    for d in range(1, NX):
        sent(GXT.at[d], S_GX + d)
    for n in range(1, 8):
        sent(GA, S_AG + n)

    @pl.when(jnp.logical_not(home))
    def _():
        sent(GA, S_AG)


def per_device(latents, grads, codebook, hard_code):
    T, W = latents.shape
    K = codebook.shape[0]
    part = T // NZ
    vmem = pl.BlockSpec(memory_space=pltpu.VMEM)
    hc = jnp.broadcast_to(hard_code[None, :], (8, T))
    scratch = [
        ((8 * T, W), BF16),
        ((8 * T, W), BF16),
        ((8, 8, T), jnp.int32),
        ((NX, K, W), BF16),
        ((W, NX * K), BF16),
        ((8, NX, K, T), F32),
        ((8, NX, K, T), F32),
        ((NX * K, 8 * T), BF16),
        ((8, NX, 8, T), F32),
        ((8, 8, T), F32),
        ((8, 8, T), F32),
        ((8, 8, T), F32),
        ((8, 8, T), F32),
        ((4, T, W), F32),
        ((4, T, W), F32),
        ((T, W), F32),
        ((4, T, W), BF16),
        ((4, T, W), BF16),
        ((T, W), F32),
        ((T, W), BF16),
        ((NZ, part, W), BF16),
        ((part, W), F32),
        ((NX, K, W), BF16),
        ((NX, K, W), BF16),
    ]
    return pl.pallas_call(
        kernel,
        out_shape=(jax.ShapeDtypeStruct((T, W), F32), jax.ShapeDtypeStruct((K, W), F32)),
        in_specs=[vmem] * 4,
        out_specs=(vmem, vmem),
        scratch_shapes=[pltpu.VMEM(s, t) for s, t in scratch]
        + [pltpu.SemaphoreType.DMA((S_ALL,)), pltpu.SemaphoreType.DMA((S_ALL,))],
        compiler_params=pltpu.CompilerParams(
            collective_id=0, has_side_effects=True, vmem_limit_bytes=60 * 2**20
        ),
    )(latents, grads, codebook, hc)


def solution(mesh):
    return jax.shard_map(
        per_device,
        mesh=mesh,
        in_specs=(P("dp", None), P("dp", None), P(("dp", "code"), None), P("dp")),
        out_specs=(P("dp", None), P(("dp", "code"), None)),
        check_vma=False,
    )
```

```python
import functools

import jax
import jax.numpy as jnp
from jax import lax
from jax.experimental import pallas as pl
from jax.experimental.pallas import tpu as pltpu
from jax.sharding import PartitionSpec as P

MESH = pl.DeviceIdType.MESH
F32 = jnp.float32
BF16 = jnp.bfloat16

NX, NY, NZ, NC = 4, 4, 8, 2
STEP = 256

S_X = 0
S_Z = 4
S_YA = 14
S_YB = 19
S_C = 24
S_ST1 = 44
S_ST2 = 52
S_ST3 = 60
S_GC = 68
S_GY = 72
S_GZ = 76
S_AG = 84
S_GX = 92
S_ALL = 96


def device(x, y, z, c):
    return ((y % 2 * NZ + z) * NC + c, x * 2 + y // 2)


def xor4(a, b):
    return (a % 2 + b % 2) % 2 + 2 * ((a // 2 + b // 2) % 2)


def nt_dot(a, b):
    return lax.dot_general(a, b, (((1,), (1,)), ((), ())), preferred_element_type=F32)


def merge(one, two):
    top = jnp.maximum(one[0], two[0])
    low = jnp.exp(one[0] - top)
    high = jnp.exp(two[0] - top)
    return (top, one[1] * low + two[1] * high, one[2] * low + two[2] * high)


def merge_all(terms):
    total = None
    for t in terms:
        rows = (t[0:1], t[1:2], t[2:3])
        total = rows if total is None else merge(total, rows)
    return total


def pack(rows):
    return jnp.concatenate([*rows, jnp.zeros((5, rows[0].shape[1]), F32)], axis=0)


def kernel(
    lat, gr, cb, hc, olat, ocb,
    LAT, GR, HC, HCL, CB, CBT, E, PU, D, H, ST, ST1, ST2, FIN,
    GCT, GCR, GYK, GYT, GYR, GZT, GZR, GXT, GXR,
    ss, rs,
):
    T, W = lat.shape
    K = cb.shape[0]
    half = T // 2
    part = T // 8
    dp = lax.axis_index("dp")
    code = lax.axis_index("code")
    c = dp % NC
    z = dp // NC % NZ
    yl = dp // (NC * NZ)
    x = code // 2
    yh = code % 2
    y = yh * 2 + yl
    zb = z // 4
    zt = xor4(z % 4, x)

    def at(dx=0, dy=0, dz=0, dc=0):
        return device((x + dx) % NX, (y + dy) % NY, (z + dz) % NZ, (c + dc) % NC)

    def diag(dz):
        z_ = (z + dz) % NZ
        return device(xor4(x, xor4(z % 4, z_ % 4)), y, z_, c)

    def copy(src, dst, dev, i, j=None):
        return pltpu.make_async_remote_copy(
            src_ref=src, dst_ref=dst, send_sem=ss.at[i], recv_sem=rs.at[i if j is None else j],
            device_id=dev, device_id_type=MESH,
        )

    def send(src, dst, dev, i, j=None):
        copy(src, dst, dev, i, j).start()

    def recv(dst, i):
        copy(dst, dst, at(dc=1), i).wait_recv()

    def sent(src, i):
        copy(src, src, at(dc=1), i).wait_send()

    def codes(j, first=0, count=K):
        return pl.ds(pl.multiple_of(j * K + first, count), count)

    yc = [(dy, dc) for dc in range(NC) for dy in range(NY) if dy or dc]
    xh = [(dx, dh) for dx in range(NX) for dh in range(2)]

    def across(dx, dh):
        return device((x + dx) % NX, (yh + dh) % 2 * 2 + yl, z, c)

    barrier = pltpu.get_barrier_semaphore()

    def greet(dev):
        pl.semaphore_signal(barrier, inc=1, device_id=dev, device_id_type=MESH)

    away = [jnp.logical_not((x == 0) & (zb == b)) for b in range(2)]
    home = (x == 0) & (zb == yh)
    for d in range(1, NX):
        greet(at(dx=d))
    for dy, dc in yc:
        greet(at(dy=dy, dc=dc))
    for d in range(1, NZ):
        greet(diag(d))
    for dx, dh in xh[1:]:
        greet(across(dx, dh))
    for b in range(2):
        @pl.when(away[b])
        def _(b=b):
            greet(device(x, y, zt + 4 * b, c))
    for zs in range(NZ):
        @pl.when(jnp.logical_not(home & (z == zs)))
        def _(zs=zs):
            greet(device(xor4(zs % 4, z % 4), zb * 2 + yl, zs, c))

    peers = NX - 1 + len(yc) + NZ - 1 + 7 + 2 + 8
    peers = peers - jnp.where(x == 0, 1, 0) - jnp.where(home, 1, 0)
    pl.semaphore_wait(barrier, peers)

    def chunk(c_, yl_, b_):
        return (c_ * 2 + yl_) * 2 + b_

    def tokens(q):
        return pl.ds(pl.multiple_of(q * T, T), T)

    def pieces(q):
        for arr in (LAT, GR):
            for h in range(2):
                yield arr.at[pl.ds(pl.multiple_of(q * T + h * half, half), half)]
        yield HC.at[q]

    HCL[...] = jnp.broadcast_to(hc[...].reshape(1, T), (8, T))
    q_own = chunk(c, yl, zb)
    own = [arr.at[pl.ds(h * half, half)] for arr in (lat, gr) for h in range(2)] + [HCL]
    dst = list(pieces(q_own))
    for p in range(5):
        for b in range(2):
            @pl.when(away[b])
            def _(p=p, b=b):
                send(own[p], dst[p], device(x, y, zt + 4 * b, c), S_Z + b * 5 + p, S_Z + zb * 5 + p)
        if p == 1:
            send(cb, CB.at[codes(x)], at(dx=1), S_X)
            send(cb, CB.at[codes(x)], at(dx=NX - 1), S_X + 1)

    @pl.when(x == 0)
    def _():
        LAT[tokens(q_own), :] = lat[...]
        GR[tokens(q_own), :] = gr[...]
        HC[q_own] = HCL[...]

    CB[codes(x), :] = cb[...]

    order = [chunk(c_, yl_, b) for c_ in (c, 1 - c) for yl_ in (yl, 1 - yl) for b in range(2)]
    refs = [list(pieces(q)) for q in order]
    left = (x + NX - 1) % NX
    right = (x + 1) % NX
    far = (x + 2) % NX
    far_refs = [CB.at[codes(left, 0, K // 2)], CB.at[codes(right, K // 2, K // 2)]]
    for p in range(5):
        for b in range(2):
            ref = refs[b][p]

            @pl.when(away[b])
            def _(ref=ref, i=S_Z + b * 5 + p):
                recv(ref, i)

            send(ref, ref, at(dy=NY - 1 if b else 1), (S_YB if b else S_YA) + p)
            send(ref, ref, at(dc=1), S_C + 5 * b + p)
        if p == 1:
            recv(CB.at[codes(left)], S_X)
            send(far_refs[0], far_refs[0], at(dx=1), S_X + 2)
            recv(CB.at[codes(right)], S_X + 1)
            send(far_refs[1], far_refs[1], at(dx=NX - 1), S_X + 3)
    recv(CB.at[codes(far, 0, K // 2)], S_X + 2)
    recv(CB.at[codes(far, K // 2, K // 2)], S_X + 3)

    def first(n):
        q = order[n]
        logit = nt_dot(CB[...], LAT[tokens(q), :])
        E[n] = logit
        PU[n] = nt_dot(CB[...], GR[tokens(q), :])
        top = jnp.max(logit, axis=0, keepdims=True)

        def rows(i, sums):
            at_ = pl.ds(pl.multiple_of(i * STEP, STEP), STEP)
            expo = jnp.exp(E[n, at_, :] - top)
            E[n, at_, :] = expo
            weighted = expo * PU[n, at_, :]
            return (
                sums[0] + jnp.sum(expo.reshape(STEP // 8, 8, T), axis=0),
                sums[1] + jnp.sum(weighted.reshape(STEP // 8, 8, T), axis=0),
            )

        zero = jnp.zeros((8, T), F32)
        total, weighted = lax.fori_loop(0, NX * K // STEP, rows, (zero, zero))
        total = jnp.sum(total, axis=0, keepdims=True)
        ST[q] = pack((top, total, jnp.sum(weighted, axis=0, keepdims=True)))

    first(0)
    first(1)
    for p in range(5):
        for b in range(2):
            ref = refs[2 + b][p]
            recv(ref, (S_YB if b else S_YA) + p)
            send(ref, ref, at(dc=1), S_C + 10 + 5 * b + p)
    first(2)
    first(3)
    for k in range(4):
        for p in range(5):
            recv(refs[4 + k][p], S_C + 5 * k + p)
    for n in range(4, 8):
        first(n)

    base = ((yl * NZ + z) * NC + c) * 8 + yh

    def hard_rows(d):
        first_code = (base + (x + d) % NX * 2) * K
        ids = first_code + lax.broadcasted_iota(jnp.int32, (K, 8 * T), 0)
        row = jnp.concatenate([HC[q][0:1] for q in range(8)], axis=1)
        hit = jnp.where(row == ids, 1.0, 0.0).astype(BF16)
        H[d] = jnp.dot(hit, GR[...], preferred_element_type=F32)

    def mine(y_, c_):
        return chunk(c_, y_ % 2, y_ // 2)

    q_me = mine(y, c)
    for dy, dc in yc:
        n = dc * NY + dy
        send(ST.at[mine((y + dy) % NY, (c + dc) % NC)], ST1.at[n], at(dy=dy, dc=dc), S_ST1 + n)
    hard_rows(2)
    for dy, dc in yc:
        recv(ST1.at[dc * NY + dy], S_ST1 + dc * NY + dy)
    ST2[0] = pack(merge_all([ST[q_me]] + [ST1[dc * NY + dy] for dy, dc in yc]))
    for d in range(1, NZ):
        send(ST2.at[0], ST2.at[d], diag(d), S_ST2 + d)
    hard_rows(1)
    hard_rows(3)
    for d in range(1, NZ):
        recv(ST2.at[d], S_ST2 + d)
    top, total, weighted = merge_all([ST2[d] for d in range(NZ)])
    FIN[q_me] = pack((top, 1.0 / total, weighted / total))
    for dy, dc in yc:
        n = dc * NY + dy
        send(FIN.at[q_me], FIN.at[q_me], at(dy=dy, dc=dc), S_ST3 + n)
    hard_rows(0)
    CBT[...] = CB[...].T
    for dy, dc in yc:
        recv(FIN.at[mine((y + NY - dy) % NY, (c + dc) % NC)], S_ST3 + dc * NY + dy)

    def latent_grad(n, q):
        fin = FIN[q]
        factor = jnp.exp(ST[q][0:1] - fin[0:1]) * fin[1:2]
        dlog = ((E[n] * factor) * (PU[n] - fin[2:3])).astype(BF16)
        D[:, tokens(q)] = dlog
        return jnp.dot(CBT[...], dlog, preferred_element_type=F32).T

    for k in range(4):
        GCT[k] = latent_grad(4 + k, order[4 + k])
        send(GCT.at[k], GCR.at[k], at(dc=1), S_GC + k)

    for d in (2, 1, 3, 0):
        y_ = (y + d) % NY
        k = (y_ + yl) % 2 * 2 + y_ // 2
        total = latent_grad(k, mine(y_, c))
        if d == 2:
            for k_ in range(4):
                recv(GCR.at[k_], S_GC + k_)
        total = total + GCR[k]
        if d:
            GYT[d] = total.astype(BF16)
            send(GYT.at[d], GYR.at[d], at(dy=d), S_GY + d)
        else:
            GYK[...] = total

    def codebook_grad(d):
        return H[d] + jnp.dot(D[codes((x + d) % NX), :], LAT[...], preferred_element_type=F32)

    def codebook_send(d):
        GXT[d] = codebook_grad(d).astype(BF16)
        send(GXT.at[d], GXR.at[d], at(dx=d), S_GX + d)

    codebook_send(2)
    codebook_send(1)

    total = GYK[...]
    for d in range(1, NY):
        recv(GYR.at[d], S_GY + d)
        total = total + GYR[d].astype(F32)
    GZT[...] = total.astype(BF16)

    def rows_of(x_, yh_):
        return pl.ds(pl.multiple_of((x_ * 2 + yh_) * part, part), part)

    rows_me = rows_of(x, yh)
    for dx, dh in xh:
        x_ = (x + dx) % NX
        yh_ = (yh + dh) % 2
        src = GZT.at[rows_of(x_, yh_)]
        dev = device(x_, yh_ * 2 + yl, zt + 4 * yh, c)
        if dx or dh:
            send(src, GZR.at[z], dev, S_GZ + dx * 2 + dh, S_GZ + z)
        else:
            @pl.when(jnp.logical_not(home))
            def _(src=src, dev=dev):
                send(src, GZR.at[z], dev, S_GZ, S_GZ + z)

            @pl.when(home)
            def _():
                GZR[z] = GZT[rows_me, :]

    codebook_send(3)
    ocb[...] = codebook_grad(0)

    for zs in range(NZ):
        @pl.when(jnp.logical_not(home & (z == zs)))
        def _(zs=zs):
            recv(GZR.at[zs], S_GZ + zs)
    total = GZR[0].astype(F32)
    for zs in range(1, NZ):
        total = total + GZR[zs].astype(F32)
    olat[rows_me, :] = total
    for dx, dh in xh[1:]:
        ref = olat.at[rows_me]
        send(ref, ref, across(dx, dh), S_AG + dx * 2 + dh)

    total = ocb[...]
    for d in range(1, NX):
        recv(GXR.at[d], S_GX + d)
        total = total + GXR[d].astype(F32)
    ocb[...] = total

    for dx, dh in xh[1:]:
        recv(olat.at[rows_of((x + NX - dx) % NX, (yh + dh) % 2)], S_AG + dx * 2 + dh)

    sent(cb, S_X)
    sent(cb, S_X + 1)
    sent(far_refs[0], S_X + 2)
    sent(far_refs[1], S_X + 3)
    for p in range(5):
        for b in range(2):
            @pl.when(away[b])
            def _(p=p, b=b):
                sent(own[p], S_Z + b * 5 + p)

        sent(refs[0][p], S_YA + p)
        sent(refs[1][p], S_YB + p)
        for k in range(4):
            sent(refs[k][p], S_C + 5 * k + p)
    for dy, dc in yc:
        n = dc * NY + dy
        sent(ST.at[0], S_ST1 + n)
        sent(FIN.at[0], S_ST3 + n)
    for d in range(1, NZ):
        sent(ST2.at[0], S_ST2 + d)
    for k in range(4):
        sent(GCT.at[k], S_GC + k)
    for d in range(1, NY):
        sent(GYT.at[d], S_GY + d)
    for d in range(1, NX):
        sent(GXT.at[d], S_GX + d)
    for n in range(1, 8):
        sent(GZT.at[pl.ds(0, part)], S_GZ + n)
        sent(olat.at[pl.ds(0, part)], S_AG + n)

    @pl.when(jnp.logical_not(home))
    def _():
        sent(GZT.at[pl.ds(0, part)], S_GZ)


def per_device(latents, grads, codebook, hard_code):
    T, W = latents.shape
    K = codebook.shape[0]
    part = T // 8
    vmem = pl.BlockSpec(memory_space=pltpu.VMEM)
    scratch = [
        ((8 * T, W), BF16),
        ((8 * T, W), BF16),
        ((8, 8, T), jnp.int32),
        ((8, T), jnp.int32),
        ((NX * K, W), BF16),
        ((W, NX * K), BF16),
        ((8, NX * K, T), F32),
        ((8, NX * K, T), F32),
        ((NX * K, 8 * T), BF16),
        ((NX, K, W), F32),
        ((8, 8, T), F32),
        ((8, 8, T), F32),
        ((8, 8, T), F32),
        ((8, 8, T), F32),
        ((4, T, W), F32),
        ((4, T, W), F32),
        ((T, W), F32),
        ((4, T, W), BF16),
        ((4, T, W), BF16),
        ((T, W), BF16),
        ((NZ, part, W), BF16),
        ((NX, K, W), BF16),
        ((NX, K, W), BF16),
    ]
    return pl.pallas_call(
        kernel,
        out_shape=(jax.ShapeDtypeStruct((T, W), F32), jax.ShapeDtypeStruct((K, W), F32)),
        in_specs=[vmem] * 4,
        out_specs=(vmem, vmem),
        scratch_shapes=[pltpu.VMEM(s, t) for s, t in scratch]
        + [pltpu.SemaphoreType.DMA((S_ALL,)), pltpu.SemaphoreType.DMA((S_ALL,))],
        compiler_params=pltpu.CompilerParams(
            collective_id=0, has_side_effects=True, vmem_limit_bytes=62 * 2**20
        ),
    )(latents, grads, codebook, hard_code)


def solution(mesh):
    return jax.shard_map(
        per_device,
        mesh=mesh,
        in_specs=(P("dp", None), P("dp", None), P(("dp", "code"), None), P("dp")),
        out_specs=(P("dp", None), P(("dp", "code"), None)),
        check_vma=False,
    )
```

```python
import functools

import jax
import jax.numpy as jnp
from jax import lax
from jax.experimental import pallas as pl
from jax.experimental.pallas import tpu as pltpu
from jax.sharding import PartitionSpec as P

MESH = pl.DeviceIdType.MESH
F32 = jnp.float32
BF16 = jnp.bfloat16

NX, NY, NZ, NC = 4, 4, 8, 2
STEP = 256

S_X = 0
S_Z = 6
S_YA = 16
S_YB = 21
S_C = 26
S_SC = 46
S_SY = 48
S_SZ = 56
S_SF = 72
S_GC = 74
S_GY = 78
S_GZ = 86
S_AG = 102
S_GX = 118
S_ALL = 122


def device(x, y, z, c):
    return ((y % 2 * NZ + z) * NC + c, x * 2 + y // 2)


def xor4(a, b):
    return (a % 2 + b % 2) % 2 + 2 * ((a // 2 + b // 2) % 2)


def nt_dot(a, b):
    return lax.dot_general(a, b, (((1,), (1,)), ((), ())), preferred_element_type=F32)


def merge(terms):
    top = terms[0]
    for t in terms[1:]:
        top = jnp.maximum(top, t)
    sums = None
    for t in terms:
        term = t * pltpu.roll(jnp.exp(t - top), 4, axis=0)
        sums = term if sums is None else sums + term
    return jnp.where(lax.broadcasted_iota(jnp.int32, top.shape, 0) < 4, top, sums)


def kernel(
    lat, gr, cb, hc, olat, ocb,
    LAT, GR, HC, HCL, CB, CBT, E, PU, D, H, ST, SC, SCR, SY, SZ, FIN,
    GCT, GCR, GYK, GYT, GYR, GZT, GZR, GA, GXT, GXR, OC,
    ss, rs, ls,
):
    T, W = lat.shape
    K = cb.shape[0]
    half = T // 2
    part = T // 16
    dp = lax.axis_index("dp")
    code = lax.axis_index("code")
    c = dp % NC
    z = dp // NC % NZ
    yl = dp // (NC * NZ)
    x = code // 2
    yh = code % 2
    y = yh * 2 + yl
    zb = z // 4
    zt = xor4(z % 4, x)

    def at(dx=0, dy=0, dz=0, dc=0):
        return device((x + dx) % NX, (y + dy) % NY, (z + dz) % NZ, (c + dc) % NC)

    def diag(dz):
        z_ = (z + dz) % NZ
        return device(xor4(x, xor4(z % 4, z_ % 4)), y, z_, c)

    def copy(src, dst, dev, i, j=None):
        return pltpu.make_async_remote_copy(
            src_ref=src, dst_ref=dst, send_sem=ss.at[i], recv_sem=rs.at[i if j is None else j],
            device_id=dev, device_id_type=MESH,
        )

    def send(src, dst, dev, i, j=None):
        copy(src, dst, dev, i, j).start()

    def recv(dst, i):
        copy(dst, dst, at(dc=1), i).wait_recv()

    def sent(src, i):
        copy(src, src, at(dc=1), i).wait_send()

    def codes(j, first=0, count=K):
        return pl.ds(pl.multiple_of(j * K + first, count), count)

    xh = [(dx, dh) for dx in range(NX) for dh in range(2)]

    def across(dx, dh):
        return device((x + dx) % NX, (yh + dh) % 2 * 2 + yl, z, c)

    barrier = pltpu.get_barrier_semaphore()

    def greet(dev):
        pl.semaphore_signal(barrier, inc=1, device_id=dev, device_id_type=MESH)

    away = [jnp.logical_not((x == 0) & (zb == b)) for b in range(2)]
    home = (x == 0) & (zb == yh)
    for d in range(1, NX):
        greet(at(dx=d))
    greet(at(dc=1))
    for d in range(1, NY):
        greet(at(dy=d))
    for d in range(1, NZ):
        greet(diag(d))
    for dx, dh in xh[1:]:
        greet(across(dx, dh))
    for b in range(2):
        @pl.when(away[b])
        def _(b=b):
            greet(device(x, y, zt + 4 * b, c))
    for zs in range(NZ):
        @pl.when(jnp.logical_not(home & (z == zs)))
        def _(zs=zs):
            greet(device(xor4(zs % 4, z % 4), zb * 2 + yl, zs, c))

    peers = NX - 1 + 1 + NY - 1 + NZ - 1 + 7 + 2 + 8
    peers = peers - jnp.where(x == 0, 1, 0) - jnp.where(home, 1, 0)
    pl.semaphore_wait(barrier, peers)

    def tile(h_, c_, yl_):
        return (h_ * 2 + c_) * 2 + yl_

    def tokens(q):
        return pl.ds(pl.multiple_of(q * T, T), T)

    def half_rows(h_, c_, yl_, b_):
        return pl.ds(pl.multiple_of(tile(h_, c_, yl_) * T + b_ * half, half), half)

    def pieces(c_, yl_, b_):
        for h_ in range(2):
            rows = half_rows(h_, c_, yl_, b_)
            yield LAT.at[rows]
            yield GR.at[rows]
        yield HC.at[(c_ * 2 + yl_) * 2 + b_]

    first_half, second_half = pl.ds(0, K // 2), pl.ds(K // 2, K // 2)
    send(cb.at[first_half], CB.at[codes(x, 0, K // 2)], at(dx=1), S_X)
    send(cb.at[second_half], CB.at[codes(x, K // 2, K // 2)], at(dx=NX - 1), S_X + 2)

    HCL[...] = jnp.broadcast_to(hc[...].reshape(1, T), (8, T))
    own = [arr.at[pl.ds(h * half, half)] for h in range(2) for arr in (lat, gr)] + [HCL]
    dst = list(pieces(c, yl, zb))
    for p in range(5):
        for b in range(2):
            @pl.when(away[b])
            def _(p=p, b=b):
                send(own[p], dst[p], device(x, y, zt + 4 * b, c), S_Z + b * 5 + p, S_Z + zb * 5 + p)
        if p == 1:
            send(cb.at[second_half], CB.at[codes(x, K // 2, K // 2)], at(dx=1), S_X + 1)
            send(cb.at[first_half], CB.at[codes(x, 0, K // 2)], at(dx=NX - 1), S_X + 3)

    def local(src, dst, i):
        return pltpu.make_async_copy(src, dst, ls.at[i])

    keep = [local(own[p], dst[p], p) for p in range(4)]
    keep_codes = local(cb, CB.at[codes(x)], 4)
    keep_codes.start()

    @pl.when(x == 0)
    def _():
        for one in keep:
            one.start()
        HC[(c * 2 + yl) * 2 + zb] = HCL[...]

    groups = [(c_, yl_) for c_ in (c, 1 - c) for yl_ in (yl, 1 - yl)]
    refs = [list(pieces(c_, yl_, b)) for c_, yl_ in groups for b in range(2)]
    left = (x + NX - 1) % NX
    right = (x + 1) % NX
    far = (x + 2) % NX
    far_refs = [CB.at[codes(left, 0, K // 2)], CB.at[codes(right, K // 2, K // 2)]]

    def from_z(p):
        for b in range(2):
            ref = refs[b][p]

            @pl.when(away[b])
            def _(ref=ref, i=S_Z + b * 5 + p):
                recv(ref, i)

            if p < 4:
                @pl.when(jnp.logical_not(away[b]))
                def _():
                    keep[p].wait()

            send(ref, ref, at(dy=NY - 1 if b else 1), (S_YB if b else S_YA) + p)
            send(ref, ref, at(dc=1), S_C + 5 * b + p)

    def from_y(p):
        for b in range(2):
            ref = refs[2 + b][p]
            recv(ref, (S_YB if b else S_YA) + p)
            send(ref, ref, at(dc=1), S_C + 10 + 5 * b + p)

    def from_core(p):
        for k in range(4):
            recv(refs[4 + k][p], S_C + 5 * k + p)

    from_z(0)
    recv(far_refs[0], S_X)
    send(far_refs[0], far_refs[0], at(dx=1), S_X + 4)
    recv(far_refs[1], S_X + 2)
    send(far_refs[1], far_refs[1], at(dx=NX - 1), S_X + 5)
    from_z(1)
    from_y(0)
    from_z(2)
    from_y(1)
    recv(CB.at[codes(left, K // 2, K // 2)], S_X + 1)
    recv(CB.at[codes(right, 0, K // 2)], S_X + 3)
    recv(CB.at[codes(far, 0, K // 2)], S_X + 4)
    recv(CB.at[codes(far, K // 2, K // 2)], S_X + 5)
    keep_codes.wait()

    def first(n):
        q = order[n]
        logit = nt_dot(CB[...], LAT[tokens(q), :])
        E[n] = logit
        PU[n] = nt_dot(CB[...], GR[tokens(q), :])
        top = jnp.max(logit, axis=0, keepdims=True)

        def rows(i, sums):
            at_ = pl.ds(pl.multiple_of(i * STEP, STEP), STEP)
            expo = jnp.exp(E[n, at_, :] - top)
            E[n, at_, :] = expo
            weighted = expo * PU[n, at_, :]
            return (
                sums[0] + jnp.sum(expo.reshape(STEP // 8, 8, T), axis=0),
                sums[1] + jnp.sum(weighted.reshape(STEP // 8, 8, T), axis=0),
            )

        zero = jnp.zeros((8, T), F32)
        total, weighted = lax.fori_loop(0, NX * K // STEP, rows, (zero, zero))
        total = jnp.sum(total, axis=0, keepdims=True)
        weighted = jnp.sum(weighted, axis=0, keepdims=True)
        ST[q] = jnp.concatenate([top, total, weighted, jnp.zeros((5, T), F32)], axis=0)

    order = [tile(h, c_, yl_) for h in range(2) for c_, yl_ in groups]

    def both(h, c_):
        one, two = ST[tile(h, c_, 0)], ST[tile(h, c_, 1)]
        tops = [one[0:1], two[0:1]]
        return jnp.concatenate([*tops, *tops, one[1:2], two[1:2], one[2:3], two[2:3]], axis=0)

    def stats_core(h):
        SC[h] = both(h, 1 - c)
        send(SC.at[h], SCR.at[h], at(dc=1), S_SC + h)

    def stats_y(h):
        mine = both(h, c)
        recv(SCR.at[h], S_SC + h)
        SY[h, 0] = merge([mine, SCR[h]])
        for d in range(1, NY):
            send(SY.at[h, 0], SY.at[h, d], at(dy=d), S_SY + 4 * h + d)

    def stats_z(h):
        for d in range(1, NY):
            recv(SY.at[h, d], S_SY + 4 * h + d)
        SZ[h, 0] = merge([SY[h, d] for d in range(NY)])
        for d in range(1, NZ):
            send(SZ.at[h, 0], SZ.at[h, d], diag(d), S_SZ + 8 * h + d)

    def stats_last(h):
        for d in range(1, NZ):
            recv(SZ.at[h, d], S_SZ + 8 * h + d)
        FIN[h, c] = merge([SZ[h, d] for d in range(NZ)])
        send(FIN.at[h, c], FIN.at[h, c], at(dc=1), S_SF + h)

    def stats_end(h):
        recv(FIN.at[h, 1 - c], S_SF + h)

    base = ((yl * NZ + z) * NC + c) * 8 + yh

    def hard_rows(d):
        first_code = (base + (x + d) % NX * 2) * K
        ids = first_code + lax.broadcasted_iota(jnp.int32, (K, 8 * T), 0)
        row = jnp.concatenate(
            [HC[g * 2 + b][0:1, h * half:(h + 1) * half] for h in range(2) for g in range(4) for b in range(2)],
            axis=1,
        )
        hit = jnp.where(row == ids, 1.0, 0.0).astype(BF16)
        H[d] = jnp.dot(hit, GR[...], preferred_element_type=F32)

    def latent_grad(n):
        q = order[n]
        pair = FIN[n // 4, q // 2 % 2]
        fin = jnp.where(q % 2 == 0, pair, pltpu.roll(pair, 7, axis=0))
        inverse = 1.0 / fin[4:5]
        factor = jnp.exp(ST[q][0:1] - fin[0:1]) * inverse
        dlog = ((E[n] * factor) * (PU[n] - fin[6:7] * inverse)).astype(BF16)
        D[:, tokens(q)] = dlog
        return jnp.dot(CBT[...], dlog, preferred_element_type=F32).T

    def latent_other(h):
        for k in range(2):
            GCT[h, k] = latent_grad(4 * h + 2 + k)
            send(GCT.at[h, k], GCR.at[h, k], at(dc=1), S_GC + 2 * h + k)

    def latent_own(h):
        for k in (1, 0):
            total = latent_grad(4 * h + k)
            recv(GCR.at[h, k], S_GC + 2 * h + k)
            GYK[h, k] = total + GCR[h, k]
            GYT[h, k] = GYK[h, k].astype(BF16)

            def part_of(b):
                return GYT.at[h, k, pl.ds(pl.multiple_of(b * half, half), half)]

            if k:
                for b in range(2):
                    dev = device(x, b * 2 + 1 - yl, z, c)
                    send(part_of(b), GYR.at[h, y], dev, S_GY + 4 * h + b, S_GY + 4 * h + y)
            else:
                send(part_of(1 - yh), GYR.at[h, y], at(dy=2), S_GY + 4 * h + 2, S_GY + 4 * h + y)

    def rows_of(x_, yh_, first=0):
        return pl.ds(pl.multiple_of(first + (x_ * 2 + yh_) * part, part), part)

    def latent_home(h):
        total = GYK[h, 0, pl.ds(pl.multiple_of(yh * half, half), half), :]
        for d in range(1, NY):
            y_ = (y + d) % NY
            recv(GYR.at[h, y_], S_GY + 4 * h + y_)
            total = total + GYR[h, y_].astype(F32)
        GZT[h] = total.astype(BF16)
        for dx, dh in xh:
            x_ = (x + dx) % NX
            yh_ = (yh + dh) % 2
            src = GZT.at[h, rows_of(x_, yh_)]
            dev = device(x_, yh_ * 2 + yl, zt + 4 * yh, c)
            if dx or dh:
                send(src, GZR.at[h, z], dev, S_GZ + 8 * h + dx * 2 + dh, S_GZ + 8 * h + z)
            else:
                @pl.when(jnp.logical_not(home))
                def _(src=src, dev=dev):
                    send(src, GZR.at[h, z], dev, S_GZ + 8 * h, S_GZ + 8 * h + z)

                @pl.when(home)
                def _():
                    GZR[h, z] = GZT[h, rows_of(x, yh), :]

    def latent_spread(h):
        for zs in range(NZ):
            @pl.when(jnp.logical_not(home & (z == zs)))
            def _(zs=zs):
                recv(GZR.at[h, zs], S_GZ + 8 * h + zs)
        total = GZR[h, 0].astype(F32)
        for zs in range(1, NZ):
            total = total + GZR[h, zs].astype(F32)
        rows = rows_of(x, yh, h * half)
        GA[h] = total
        for dx, dh in xh[1:]:
            send(GA.at[h], olat.at[rows], across(dx, dh), S_AG + 8 * h + dx * 2 + dh)
        local(GA.at[h], olat.at[rows], 5 + h).start()

    def codebook_grad(d):
        return H[d] + jnp.dot(D[codes((x + d) % NX), :], LAT[...], preferred_element_type=F32)

    def codebook_send(d):
        GXT[d] = codebook_grad(d).astype(BF16)
        send(GXT.at[d], GXR.at[d], at(dx=d), S_GX + d)

    first(0)
    from_z(3)
    from_core(0)
    from_core(1)
    first(1)
    from_y(2)
    from_z(4)
    first(2)
    first(3)
    stats_core(0)
    from_y(3)
    from_y(4)
    first(4)
    stats_y(0)
    first(5)
    for p in range(2, 5):
        from_core(p)
    first(6)
    stats_z(0)
    first(7)
    stats_core(1)
    hard_rows(2)
    stats_y(1)
    hard_rows(1)
    hard_rows(3)
    CBT[...] = CB[...].T
    stats_last(0)
    stats_z(1)
    stats_end(0)
    latent_other(0)
    latent_own(0)
    hard_rows(0)
    stats_last(1)
    stats_end(1)
    latent_other(1)
    latent_home(0)
    latent_own(1)
    codebook_send(2)
    latent_home(1)
    latent_spread(0)
    codebook_send(1)
    codebook_send(3)
    latent_spread(1)
    total = codebook_grad(0)
    for d in range(1, NX):
        recv(GXR.at[d], S_GX + d)
        total = total + GXR[d].astype(F32)
    OC[...] = total
    out = local(OC, ocb, 7)
    out.start()

    for h in range(2):
        for dx, dh in xh[1:]:
            rows = rows_of((x + NX - dx) % NX, (yh + dh) % 2, h * half)
            recv(olat.at[rows], S_AG + 8 * h + dx * 2 + dh)
        local(GA.at[h], olat.at[rows_of(x, yh, h * half)], 5 + h).wait()
    out.wait()

    for n in range(4):
        sent(cb.at[first_half], S_X + n)
    sent(far_refs[0], S_X + 4)
    sent(far_refs[1], S_X + 5)
    for p in range(5):
        for b in range(2):
            @pl.when(away[b])
            def _(p=p, b=b):
                sent(own[p], S_Z + b * 5 + p)

        sent(refs[0][p], S_YA + p)
        sent(refs[1][p], S_YB + p)
        for k in range(4):
            sent(refs[k][p], S_C + 5 * k + p)
    for h in range(2):
        sent(SC.at[h], S_SC + h)
        sent(SC.at[h], S_SF + h)
        for d in range(1, NY):
            sent(SC.at[h], S_SY + 4 * h + d)
        for d in range(1, NZ):
            sent(SC.at[h], S_SZ + 8 * h + d)
        for k in range(2):
            sent(GCT.at[h, k], S_GC + 2 * h + k)
        for n in range(3):
            sent(GYR.at[0, 0], S_GY + 4 * h + n)
        for n in range(1, 8):
            sent(GZR.at[0, 0], S_GZ + 8 * h + n)
            sent(GA.at[h], S_AG + 8 * h + n)

        @pl.when(jnp.logical_not(home))
        def _(h=h):
            sent(GZR.at[0, 0], S_GZ + 8 * h)
    for d in range(1, NX):
        sent(GXT.at[d], S_GX + d)


def per_device(latents, grads, codebook, hard_code):
    T, W = latents.shape
    K = codebook.shape[0]
    part = T // 16
    half = T // 2
    vmem = pl.BlockSpec(memory_space=pltpu.VMEM)
    hbm = pl.BlockSpec(memory_space=pl.ANY)
    scratch = [
        ((8 * T, W), BF16),
        ((8 * T, W), BF16),
        ((8, 8, T), jnp.int32),
        ((8, T), jnp.int32),
        ((NX * K, W), BF16),
        ((W, NX * K), BF16),
        ((8, NX * K, T), F32),
        ((8, NX * K, T), F32),
        ((NX * K, 8 * T), BF16),
        ((NX, K, W), F32),
        ((8, 8, T), F32),
        ((2, 8, T), F32),
        ((2, 8, T), F32),
        ((2, NY, 8, T), F32),
        ((2, NZ, 8, T), F32),
        ((2, 2, 8, T), F32),
        ((2, 2, T, W), F32),
        ((2, 2, T, W), F32),
        ((2, 2, T, W), F32),
        ((2, 2, T, W), BF16),
        ((2, 4, half, W), BF16),
        ((2, half, W), BF16),
        ((2, NZ, part, W), BF16),
        ((2, part, W), F32),
        ((NX, K, W), BF16),
        ((NX, K, W), BF16),
        ((K, W), F32),
    ]
    return pl.pallas_call(
        kernel,
        out_shape=(jax.ShapeDtypeStruct((T, W), F32), jax.ShapeDtypeStruct((K, W), F32)),
        in_specs=[hbm, hbm, hbm, vmem],
        out_specs=(hbm, hbm),
        scratch_shapes=[pltpu.VMEM(s, t) for s, t in scratch]
        + [pltpu.SemaphoreType.DMA((n,)) for n in (S_ALL, S_ALL, 8)],
        compiler_params=pltpu.CompilerParams(
            collective_id=0, has_side_effects=True, vmem_limit_bytes=62 * 2**20
        ),
    )(latents, grads, codebook, hard_code)


def solution(mesh):
    return jax.shard_map(
        per_device,
        mesh=mesh,
        in_specs=(P("dp", None), P("dp", None), P(("dp", "code"), None), P("dp")),
        out_specs=(P("dp", None), P(("dp", "code"), None)),
        check_vma=False,
    )
```

```python
import functools

import jax
import jax.numpy as jnp
from jax import lax
from jax.experimental import pallas as pl
from jax.experimental.pallas import tpu as pltpu
from jax.sharding import PartitionSpec as P

MESH = pl.DeviceIdType.MESH
F32 = jnp.float32
BF16 = jnp.bfloat16

NX, NY, NZ, NC = 4, 4, 8, 2
STEP = 256

S_X = 0
S_Z = 6
S_YA = 16
S_YB = 21
S_C = 26
S_SC = 46
S_SY = 48
S_SZ = 56
S_SF = 72
S_GC = 74
S_GY = 78
S_GZ = 86
S_AG = 102
S_GX = 118
S_ALL = 122


def device(x, y, z, c):
    return ((y % 2 * NZ + z) * NC + c, x * 2 + y // 2)


def xor4(a, b):
    return (a % 2 + b % 2) % 2 + 2 * ((a // 2 + b // 2) % 2)


def nt_dot(a, b):
    return lax.dot_general(a, b, (((1,), (1,)), ((), ())), preferred_element_type=F32)


def merge(terms):
    top = terms[0]
    for t in terms[1:]:
        top = jnp.maximum(top, t)
    sums = None
    for t in terms:
        term = t * pltpu.roll(jnp.exp(t - top), 4, axis=0)
        sums = term if sums is None else sums + term
    return jnp.where(lax.broadcasted_iota(jnp.int32, top.shape, 0) < 4, top, sums)


def kernel(
    lat, gr, cb, hc, olat, ocb,
    LAT, GR, HC, HCL, CB, CBT, E, PU, D, H, ST, SC, SCR, SY, SZ, FIN,
    GCT, GCR, GYK, GYT, GYR, GZT, GZR, GA, GXT, GXR, OC,
    ss, rs, ls,
):
    T, W = lat.shape
    K = cb.shape[0]
    half = T // 2
    part = T // 16
    dp = lax.axis_index("dp")
    code = lax.axis_index("code")
    c = dp % NC
    z = dp // NC % NZ
    yl = dp // (NC * NZ)
    x = code // 2
    yh = code % 2
    y = yh * 2 + yl
    zb = z // 4
    zt = xor4(z % 4, x)

    def at(dx=0, dy=0, dz=0, dc=0):
        return device((x + dx) % NX, (y + dy) % NY, (z + dz) % NZ, (c + dc) % NC)

    def diag(dz):
        z_ = (z + dz) % NZ
        return device(xor4(x, xor4(z % 4, z_ % 4)), y, z_, c)

    def copy(src, dst, dev, i, j=None):
        return pltpu.make_async_remote_copy(
            src_ref=src, dst_ref=dst, send_sem=ss.at[i], recv_sem=rs.at[i if j is None else j],
            device_id=dev, device_id_type=MESH,
        )

    def send(src, dst, dev, i, j=None):
        copy(src, dst, dev, i, j).start()

    def recv(dst, i):
        copy(dst, dst, at(dc=1), i).wait_recv()

    def sent(src, i):
        copy(src, src, at(dc=1), i).wait_send()

    def codes(j, first=0, count=K):
        return pl.ds(pl.multiple_of(j * K + first, count), count)

    xh = [(dx, dh) for dx in range(NX) for dh in range(2)]

    def across(dx, dh):
        return device((x + dx) % NX, (yh + dh) % 2 * 2 + yl, z, c)

    barrier = pltpu.get_barrier_semaphore()

    def greet(dev):
        pl.semaphore_signal(barrier, inc=1, device_id=dev, device_id_type=MESH)

    away = [jnp.logical_not((x == 0) & (zb == b)) for b in range(2)]
    home = (x == 0) & (zb == yh)
    for d in range(1, NX):
        greet(at(dx=d))
    greet(at(dc=1))
    for d in range(1, NY):
        greet(at(dy=d))
    for d in range(1, NZ):
        greet(diag(d))
    for dx, dh in xh[1:]:
        greet(across(dx, dh))
    for b in range(2):
        @pl.when(away[b])
        def _(b=b):
            greet(device(x, y, zt + 4 * b, c))
    for zs in range(NZ):
        @pl.when(jnp.logical_not(home & (z == zs)))
        def _(zs=zs):
            greet(device(xor4(zs % 4, z % 4), zb * 2 + yl, zs, c))

    peers = NX - 1 + 1 + NY - 1 + NZ - 1 + 7 + 2 + 8
    peers = peers - jnp.where(x == 0, 1, 0) - jnp.where(home, 1, 0)
    pl.semaphore_wait(barrier, peers)

    def tile(h_, c_, yl_):
        return (h_ * 2 + c_) * 2 + yl_

    def tokens(q):
        return pl.ds(pl.multiple_of(q * T, T), T)

    def half_rows(h_, c_, yl_, b_):
        return pl.ds(pl.multiple_of(tile(h_, c_, yl_) * T + b_ * half, half), half)

    def pieces(c_, yl_, b_):
        for h_ in range(2):
            rows = half_rows(h_, c_, yl_, b_)
            yield LAT.at[rows]
            yield GR.at[rows]
        yield HC.at[(c_ * 2 + yl_) * 2 + b_]

    first_half, second_half = pl.ds(0, K // 2), pl.ds(K // 2, K // 2)
    send(cb.at[first_half], CB.at[codes(x, 0, K // 2)], at(dx=1), S_X)
    send(cb.at[second_half], CB.at[codes(x, K // 2, K // 2)], at(dx=NX - 1), S_X + 2)

    HCL[...] = jnp.broadcast_to(hc[...].reshape(1, T), (8, T))
    own = [arr.at[pl.ds(h * half, half)] for h in range(2) for arr in (lat, gr)] + [HCL]
    dst = list(pieces(c, yl, zb))
    for p in range(5):
        for b in range(2):
            @pl.when(away[b])
            def _(p=p, b=b):
                send(own[p], dst[p], device(x, y, zt + 4 * b, c), S_Z + b * 5 + p, S_Z + zb * 5 + p)
        if p == 1:
            send(cb.at[second_half], CB.at[codes(x, K // 2, K // 2)], at(dx=1), S_X + 1)
            send(cb.at[first_half], CB.at[codes(x, 0, K // 2)], at(dx=NX - 1), S_X + 3)

    def local(src, dst, i):
        return pltpu.make_async_copy(src, dst, ls.at[i])

    keep = [local(own[p], dst[p], p) for p in range(4)]
    keep_codes = local(cb, CB.at[codes(x)], 4)
    keep_codes.start()

    @pl.when(x == 0)
    def _():
        for one in keep:
            one.start()
        HC[(c * 2 + yl) * 2 + zb] = HCL[...]

    groups = [(c_, yl_) for c_ in (c, 1 - c) for yl_ in (yl, 1 - yl)]
    refs = [list(pieces(c_, yl_, b)) for c_, yl_ in groups for b in range(2)]
    left = (x + NX - 1) % NX
    right = (x + 1) % NX
    far = (x + 2) % NX
    far_refs = [CB.at[codes(left, 0, K // 2)], CB.at[codes(right, K // 2, K // 2)]]

    def from_z(p):
        for b in range(2):
            ref = refs[b][p]

            @pl.when(away[b])
            def _(ref=ref, i=S_Z + b * 5 + p):
                recv(ref, i)

            if p < 4:
                @pl.when(jnp.logical_not(away[b]))
                def _():
                    keep[p].wait()

            send(ref, ref, at(dy=NY - 1 if b else 1), (S_YB if b else S_YA) + p)
            send(ref, ref, at(dc=1), S_C + 5 * b + p)

    def from_y(p):
        for b in range(2):
            ref = refs[2 + b][p]
            recv(ref, (S_YB if b else S_YA) + p)
            send(ref, ref, at(dc=1), S_C + 10 + 5 * b + p)

    def from_core(p):
        for k in range(4):
            recv(refs[4 + k][p], S_C + 5 * k + p)

    from_z(0)
    recv(far_refs[0], S_X)
    send(far_refs[0], far_refs[0], at(dx=1), S_X + 4)
    recv(far_refs[1], S_X + 2)
    send(far_refs[1], far_refs[1], at(dx=NX - 1), S_X + 5)
    from_z(1)
    from_y(0)
    from_z(2)
    from_y(1)
    recv(CB.at[codes(left, K // 2, K // 2)], S_X + 1)
    recv(CB.at[codes(right, 0, K // 2)], S_X + 3)
    recv(CB.at[codes(far, 0, K // 2)], S_X + 4)
    recv(CB.at[codes(far, K // 2, K // 2)], S_X + 5)
    keep_codes.wait()

    def first(n):
        q = order[n]
        logit = nt_dot(CB[...], LAT[tokens(q), :])
        E[n] = logit
        PU[n] = nt_dot(CB[...], GR[tokens(q), :])
        top = jnp.max(logit, axis=0, keepdims=True)

        def rows(i, sums):
            at_ = pl.ds(pl.multiple_of(i * STEP, STEP), STEP)
            expo = jnp.exp(E[n, at_, :] - top)
            E[n, at_, :] = expo
            weighted = expo * PU[n, at_, :]
            return (
                sums[0] + jnp.sum(expo.reshape(STEP // 8, 8, T), axis=0),
                sums[1] + jnp.sum(weighted.reshape(STEP // 8, 8, T), axis=0),
            )

        zero = jnp.zeros((8, T), F32)
        total, weighted = lax.fori_loop(0, NX * K // STEP, rows, (zero, zero))
        total = jnp.sum(total, axis=0, keepdims=True)
        weighted = jnp.sum(weighted, axis=0, keepdims=True)
        ST[q] = jnp.concatenate([top, total, weighted, jnp.zeros((5, T), F32)], axis=0)

    order = [tile(h, c_, yl_) for h in range(2) for c_, yl_ in groups]

    def both(h, c_):
        one, two = ST[tile(h, c_, 0)], ST[tile(h, c_, 1)]
        tops = [one[0:1], two[0:1]]
        return jnp.concatenate([*tops, *tops, one[1:2], two[1:2], one[2:3], two[2:3]], axis=0)

    def stats_core(h):
        SC[h] = both(h, 1 - c)
        send(SC.at[h], SCR.at[h], at(dc=1), S_SC + h)

    def stats_y(h):
        mine = both(h, c)
        recv(SCR.at[h], S_SC + h)
        SY[h, 0] = merge([mine, SCR[h]])
        for d in range(1, NY):
            send(SY.at[h, 0], SY.at[h, d], at(dy=d), S_SY + 4 * h + d)

    def stats_z(h):
        for d in range(1, NY):
            recv(SY.at[h, d], S_SY + 4 * h + d)
        SZ[h, 0] = merge([SY[h, d] for d in range(NY)])
        for d in range(1, NZ):
            send(SZ.at[h, 0], SZ.at[h, d], diag(d), S_SZ + 8 * h + d)

    def stats_last(h):
        for d in range(1, NZ):
            recv(SZ.at[h, d], S_SZ + 8 * h + d)
        FIN[h, c] = merge([SZ[h, d] for d in range(NZ)])
        send(FIN.at[h, c], FIN.at[h, c], at(dc=1), S_SF + h)

    def stats_end(h):
        recv(FIN.at[h, 1 - c], S_SF + h)

    base = ((yl * NZ + z) * NC + c) * 8 + yh

    def hard_rows(d):
        first_code = (base + (x + d) % NX * 2) * K
        ids = first_code + lax.broadcasted_iota(jnp.int32, (K, 8 * T), 0)
        row = jnp.concatenate(
            [HC[g * 2 + b][0:1, h * half:(h + 1) * half] for h in range(2) for g in range(4) for b in range(2)],
            axis=1,
        )
        hit = jnp.where(row == ids, 1.0, 0.0).astype(BF16)
        H[d] = jnp.dot(hit, GR[...], preferred_element_type=F32)

    def latent_grad(n):
        q = order[n]
        pair = FIN[n // 4, q // 2 % 2]
        fin = jnp.where(q % 2 == 0, pair, pltpu.roll(pair, 7, axis=0))
        inverse = 1.0 / fin[4:5]
        factor = jnp.exp(ST[q][0:1] - fin[0:1]) * inverse
        dlog = ((E[n] * factor) * (PU[n] - fin[6:7] * inverse)).astype(BF16)
        D[:, tokens(q)] = dlog
        return jnp.dot(CBT[...], dlog, preferred_element_type=F32).T

    def latent_other(h):
        for k in range(2):
            GCT[h, k] = latent_grad(4 * h + 2 + k)
            send(GCT.at[h, k], GCR.at[h, k], at(dc=1), S_GC + 2 * h + k)

    def latent_own(h):
        for k in (1, 0):
            total = latent_grad(4 * h + k)
            recv(GCR.at[h, k], S_GC + 2 * h + k)
            GYK[h, k] = total + GCR[h, k]
            GYT[h, k] = GYK[h, k].astype(BF16)

            def part_of(b):
                return GYT.at[h, k, pl.ds(pl.multiple_of(b * half, half), half)]

            if k:
                for b in range(2):
                    dev = device(x, b * 2 + 1 - yl, z, c)
                    send(part_of(b), GYR.at[h, y], dev, S_GY + 4 * h + b, S_GY + 4 * h + y)
            else:
                send(part_of(1 - yh), GYR.at[h, y], at(dy=2), S_GY + 4 * h + 2, S_GY + 4 * h + y)

    def rows_of(x_, yh_, first=0):
        return pl.ds(pl.multiple_of(first + (x_ * 2 + yh_) * part, part), part)

    def latent_home(h):
        total = GYK[h, 0, pl.ds(pl.multiple_of(yh * half, half), half), :]
        for d in range(1, NY):
            y_ = (y + d) % NY
            recv(GYR.at[h, y_], S_GY + 4 * h + y_)
            total = total + GYR[h, y_].astype(F32)
        GZT[h] = total.astype(BF16)
        for dx, dh in xh:
            x_ = (x + dx) % NX
            yh_ = (yh + dh) % 2
            src = GZT.at[h, rows_of(x_, yh_)]
            dev = device(x_, yh_ * 2 + yl, zt + 4 * yh, c)
            if dx or dh:
                send(src, GZR.at[h, z], dev, S_GZ + 8 * h + dx * 2 + dh, S_GZ + 8 * h + z)
            else:
                @pl.when(jnp.logical_not(home))
                def _(src=src, dev=dev):
                    send(src, GZR.at[h, z], dev, S_GZ + 8 * h, S_GZ + 8 * h + z)

                @pl.when(home)
                def _():
                    GZR[h, z] = GZT[h, rows_of(x, yh), :]

    def latent_spread(h):
        for zs in range(NZ):
            @pl.when(jnp.logical_not(home & (z == zs)))
            def _(zs=zs):
                recv(GZR.at[h, zs], S_GZ + 8 * h + zs)
        total = GZR[h, 0].astype(F32)
        for zs in range(1, NZ):
            total = total + GZR[h, zs].astype(F32)
        rows = rows_of(x, yh, h * half)
        GA[h] = total
        for dx, dh in xh[1:]:
            send(GA.at[h], olat.at[rows], across(dx, dh), S_AG + 8 * h + dx * 2 + dh)
        local(GA.at[h], olat.at[rows], 5 + h).start()

    def codebook_grad(d):
        return H[d] + jnp.dot(D[codes((x + d) % NX), :], LAT[...], preferred_element_type=F32)

    def codebook_far():
        GXT[2] = codebook_grad(2).astype(BF16)
        send(GXT.at[2, first_half], GXR.at[2, first_half], at(dx=1), S_GX)
        send(GXT.at[2, second_half], GXR.at[2, second_half], at(dx=3), S_GX + 2)

    def codebook_send(d):
        rows = first_half if d == 1 else second_half
        OC[...] = codebook_grad(d)
        recv(GXR.at[2, rows], S_GX + d - 1)
        OC[rows, :] = OC[rows, :] + GXR[2, rows, :].astype(F32)
        GXT[d] = OC[...].astype(BF16)
        send(GXT.at[d], GXR.at[d], at(dx=d), S_GX + d)

    first(0)
    from_z(3)
    from_core(0)
    from_core(1)
    first(1)
    from_y(2)
    from_z(4)
    first(2)
    first(3)
    stats_core(0)
    from_y(3)
    from_y(4)
    first(4)
    stats_y(0)
    first(5)
    for p in range(2, 5):
        from_core(p)
    first(6)
    stats_z(0)
    first(7)
    stats_core(1)
    hard_rows(2)
    stats_y(1)
    hard_rows(1)
    hard_rows(3)
    CBT[...] = CB[...].T
    stats_last(0)
    stats_z(1)
    stats_end(0)
    latent_other(0)
    latent_own(0)
    hard_rows(0)
    stats_last(1)
    stats_end(1)
    latent_other(1)
    latent_home(0)
    latent_own(1)
    codebook_far()
    latent_home(1)
    latent_spread(0)
    codebook_send(1)
    codebook_send(3)
    latent_spread(1)
    total = codebook_grad(0)
    for d in (1, 3):
        recv(GXR.at[d], S_GX + d)
        total = total + GXR[d].astype(F32)
    OC[...] = total
    out = local(OC, ocb, 7)
    out.start()

    for h in range(2):
        for dx, dh in xh[1:]:
            rows = rows_of((x + NX - dx) % NX, (yh + dh) % 2, h * half)
            recv(olat.at[rows], S_AG + 8 * h + dx * 2 + dh)
        local(GA.at[h], olat.at[rows_of(x, yh, h * half)], 5 + h).wait()
    out.wait()

    for n in range(4):
        sent(cb.at[first_half], S_X + n)
    sent(far_refs[0], S_X + 4)
    sent(far_refs[1], S_X + 5)
    for p in range(5):
        for b in range(2):
            @pl.when(away[b])
            def _(p=p, b=b):
                sent(own[p], S_Z + b * 5 + p)

        sent(refs[0][p], S_YA + p)
        sent(refs[1][p], S_YB + p)
        for k in range(4):
            sent(refs[k][p], S_C + 5 * k + p)
    for h in range(2):
        sent(SC.at[h], S_SC + h)
        sent(SC.at[h], S_SF + h)
        for d in range(1, NY):
            sent(SC.at[h], S_SY + 4 * h + d)
        for d in range(1, NZ):
            sent(SC.at[h], S_SZ + 8 * h + d)
        for k in range(2):
            sent(GCT.at[h, k], S_GC + 2 * h + k)
        for n in range(3):
            sent(GYR.at[0, 0], S_GY + 4 * h + n)
        for n in range(1, 8):
            sent(GZR.at[0, 0], S_GZ + 8 * h + n)
            sent(GA.at[h], S_AG + 8 * h + n)

        @pl.when(jnp.logical_not(home))
        def _(h=h):
            sent(GZR.at[0, 0], S_GZ + 8 * h)
    for d in (1, 3):
        sent(GXT.at[2, first_half], S_GX + d - 1)
        sent(GXT.at[d], S_GX + d)


def per_device(latents, grads, codebook, hard_code):
    T, W = latents.shape
    K = codebook.shape[0]
    part = T // 16
    half = T // 2
    vmem = pl.BlockSpec(memory_space=pltpu.VMEM)
    hbm = pl.BlockSpec(memory_space=pl.ANY)
    scratch = [
        ((8 * T, W), BF16),
        ((8 * T, W), BF16),
        ((8, 8, T), jnp.int32),
        ((8, T), jnp.int32),
        ((NX * K, W), BF16),
        ((W, NX * K), BF16),
        ((8, NX * K, T), F32),
        ((8, NX * K, T), F32),
        ((NX * K, 8 * T), BF16),
        ((NX, K, W), F32),
        ((8, 8, T), F32),
        ((2, 8, T), F32),
        ((2, 8, T), F32),
        ((2, NY, 8, T), F32),
        ((2, NZ, 8, T), F32),
        ((2, 2, 8, T), F32),
        ((2, 2, T, W), F32),
        ((2, 2, T, W), F32),
        ((2, 2, T, W), F32),
        ((2, 2, T, W), BF16),
        ((2, 4, half, W), BF16),
        ((2, half, W), BF16),
        ((2, NZ, part, W), BF16),
        ((2, part, W), F32),
        ((NX, K, W), BF16),
        ((NX, K, W), BF16),
        ((K, W), F32),
    ]
    return pl.pallas_call(
        kernel,
        out_shape=(jax.ShapeDtypeStruct((T, W), F32), jax.ShapeDtypeStruct((K, W), F32)),
        in_specs=[hbm, hbm, hbm, vmem],
        out_specs=(hbm, hbm),
        scratch_shapes=[pltpu.VMEM(s, t) for s, t in scratch]
        + [pltpu.SemaphoreType.DMA((n,)) for n in (S_ALL, S_ALL, 8)],
        compiler_params=pltpu.CompilerParams(
            collective_id=0, has_side_effects=True, vmem_limit_bytes=62 * 2**20
        ),
    )(latents, grads, codebook, hard_code)


def solution(mesh):
    return jax.shard_map(
        per_device,
        mesh=mesh,
        in_specs=(P("dp", None), P("dp", None), P(("dp", "code"), None), P("dp")),
        out_specs=(P("dp", None), P(("dp", "code"), None)),
        check_vma=False,
    )
```

```python
import functools

import jax
import jax.numpy as jnp
from jax import lax
from jax.experimental import pallas as pl
from jax.experimental.pallas import tpu as pltpu
from jax.sharding import PartitionSpec as P

MESH = pl.DeviceIdType.MESH
F32 = jnp.float32
BF16 = jnp.bfloat16

NX, NY, NZ, NC = 4, 4, 8, 2
STEP = 256

S_X = 0
S_Z = 6
S_YA = 16
S_YB = 21
S_C = 26
S_SC = 46
S_SY = 48
S_SZ = 56
S_SF = 72
S_GC = 74
S_GY = 78
S_GZ = 86
S_AG = 102
S_GX = 118
S_ALL = 122


def device(x, y, z, c):
    return ((y % 2 * NZ + z) * NC + c, x * 2 + y // 2)


def xor4(a, b):
    return (a % 2 + b % 2) % 2 + 2 * ((a // 2 + b // 2) % 2)


def nt_dot(a, b):
    return lax.dot_general(a, b, (((1,), (1,)), ((), ())), preferred_element_type=F32)


def merge(terms):
    top = terms[0]
    for t in terms[1:]:
        top = jnp.maximum(top, t)
    sums = None
    for t in terms:
        term = t * pltpu.roll(jnp.exp(t - top), 4, axis=0)
        sums = term if sums is None else sums + term
    return jnp.where(lax.broadcasted_iota(jnp.int32, top.shape, 0) < 4, top, sums)


def kernel(
    lat, gr, cb, hc, olat, ocb,
    LAT, GR, HC, HCL, CB, CBT, E, PU, D, H, ST, SC, SCR, SY, SZ, FIN,
    GCT, GCR, GYK, GYT, GYR, GZT, GZR, GA, GXT, GXR, OC,
    ss, rs, ls,
):
    T, W = lat.shape
    K = cb.shape[0]
    half = T // 2
    part = T // 16
    dp = lax.axis_index("dp")
    code = lax.axis_index("code")
    c = dp % NC
    z = dp // NC % NZ
    yl = dp // (NC * NZ)
    x = code // 2
    yh = code % 2
    y = yh * 2 + yl
    zb = z // 4
    zt = xor4(z % 4, x)

    def at(dx=0, dy=0, dz=0, dc=0):
        return device((x + dx) % NX, (y + dy) % NY, (z + dz) % NZ, (c + dc) % NC)

    def diag(dz):
        z_ = (z + dz) % NZ
        return device(xor4(x, xor4(z % 4, z_ % 4)), y, z_, c)

    def copy(src, dst, dev, i, j=None):
        return pltpu.make_async_remote_copy(
            src_ref=src, dst_ref=dst, send_sem=ss.at[i], recv_sem=rs.at[i if j is None else j],
            device_id=dev, device_id_type=MESH,
        )

    def send(src, dst, dev, i, j=None):
        copy(src, dst, dev, i, j).start()

    def recv(dst, i):
        copy(dst, dst, at(dc=1), i).wait_recv()

    def sent(src, i):
        copy(src, src, at(dc=1), i).wait_send()

    def codes(j, first=0, count=K):
        return pl.ds(pl.multiple_of(j * K + first, count), count)

    xh = [(dx, dh) for dx in range(NX) for dh in range(2)]

    def across(dx, dh):
        return device((x + dx) % NX, (yh + dh) % 2 * 2 + yl, z, c)

    barrier = pltpu.get_barrier_semaphore()

    def greet(dev):
        pl.semaphore_signal(barrier, inc=1, device_id=dev, device_id_type=MESH)

    away = [jnp.logical_not((x == 0) & (zb == b)) for b in range(2)]
    home = (x == 0) & (zb == yh)
    for d in range(1, NX):
        greet(at(dx=d))
    greet(at(dc=1))
    for d in range(1, NY):
        greet(at(dy=d))
    for d in range(1, NZ):
        greet(diag(d))
    for dx, dh in xh[1:]:
        greet(across(dx, dh))
    for b in range(2):
        @pl.when(away[b])
        def _(b=b):
            greet(device(x, y, zt + 4 * b, c))
    for zs in range(NZ):
        @pl.when(jnp.logical_not(home & (z == zs)))
        def _(zs=zs):
            greet(device(xor4(zs % 4, z % 4), zb * 2 + yl, zs, c))

    peers = NX - 1 + 1 + NY - 1 + NZ - 1 + 7 + 2 + 8
    peers = peers - jnp.where(x == 0, 1, 0) - jnp.where(home, 1, 0)
    pl.semaphore_wait(barrier, peers)

    def tile(h_, c_, yl_):
        return (h_ * 2 + c_) * 2 + yl_

    def tokens(q):
        return pl.ds(pl.multiple_of(q * T, T), T)

    def half_rows(h_, c_, yl_, b_):
        return pl.ds(pl.multiple_of(tile(h_, c_, yl_) * T + b_ * half, half), half)

    def pieces(c_, yl_, b_):
        for h_ in range(2):
            rows = half_rows(h_, c_, yl_, b_)
            yield LAT.at[rows]
            yield GR.at[rows]
        yield HC.at[(c_ * 2 + yl_) * 2 + b_]

    first_half, second_half = pl.ds(0, K // 2), pl.ds(K // 2, K // 2)
    send(cb.at[first_half], CB.at[codes(x, 0, K // 2)], at(dx=1), S_X)
    send(cb.at[second_half], CB.at[codes(x, K // 2, K // 2)], at(dx=NX - 1), S_X + 2)

    HCL[...] = jnp.broadcast_to(hc[...].reshape(1, T), (8, T))
    own = [arr.at[pl.ds(h * half, half)] for h in range(2) for arr in (lat, gr)] + [HCL]
    dst = list(pieces(c, yl, zb))
    for p in range(5):
        for b in range(2):
            @pl.when(away[b])
            def _(p=p, b=b):
                send(own[p], dst[p], device(x, y, zt + 4 * b, c), S_Z + b * 5 + p, S_Z + zb * 5 + p)
        if p == 1:
            send(cb.at[second_half], CB.at[codes(x, K // 2, K // 2)], at(dx=1), S_X + 1)
            send(cb.at[first_half], CB.at[codes(x, 0, K // 2)], at(dx=NX - 1), S_X + 3)

    def local(src, dst, i):
        return pltpu.make_async_copy(src, dst, ls.at[i])

    keep = [local(own[p], dst[p], p) for p in range(4)]
    keep_codes = local(cb, CB.at[codes(x)], 4)
    keep_codes.start()

    @pl.when(x == 0)
    def _():
        for one in keep:
            one.start()
        HC[(c * 2 + yl) * 2 + zb] = HCL[...]

    groups = [(c_, yl_) for c_ in (c, 1 - c) for yl_ in (yl, 1 - yl)]
    refs = [list(pieces(c_, yl_, b)) for c_, yl_ in groups for b in range(2)]
    left = (x + NX - 1) % NX
    right = (x + 1) % NX
    far = (x + 2) % NX
    far_refs = [CB.at[codes(left, 0, K // 2)], CB.at[codes(right, K // 2, K // 2)]]

    def from_z(p):
        for b in range(2):
            ref = refs[b][p]

            @pl.when(away[b])
            def _(ref=ref, i=S_Z + b * 5 + p):
                recv(ref, i)

            if p < 4:
                @pl.when(jnp.logical_not(away[b]))
                def _():
                    keep[p].wait()

            send(ref, ref, at(dy=NY - 1 if b else 1), (S_YB if b else S_YA) + p)
            send(ref, ref, at(dc=1), S_C + 5 * b + p)

    def from_y(p):
        for b in range(2):
            ref = refs[2 + b][p]
            recv(ref, (S_YB if b else S_YA) + p)
            send(ref, ref, at(dc=1), S_C + 10 + 5 * b + p)

    def from_core(p):
        for k in range(4):
            recv(refs[4 + k][p], S_C + 5 * k + p)

    from_z(0)
    recv(far_refs[0], S_X)
    send(far_refs[0], far_refs[0], at(dx=1), S_X + 4)
    recv(far_refs[1], S_X + 2)
    send(far_refs[1], far_refs[1], at(dx=NX - 1), S_X + 5)
    from_z(1)
    from_y(0)
    from_z(2)
    from_y(1)
    recv(CB.at[codes(left, K // 2, K // 2)], S_X + 1)
    recv(CB.at[codes(right, 0, K // 2)], S_X + 3)
    recv(CB.at[codes(far, 0, K // 2)], S_X + 4)
    recv(CB.at[codes(far, K // 2, K // 2)], S_X + 5)
    keep_codes.wait()

    def first(n):
        q = order[n]
        logit = nt_dot(CB[...], LAT[tokens(q), :])
        E[n] = logit
        PU[n] = nt_dot(CB[...], GR[tokens(q), :])
        top = jnp.max(logit, axis=0, keepdims=True)

        def rows(i, sums):
            at_ = pl.ds(pl.multiple_of(i * STEP, STEP), STEP)
            expo = jnp.exp(E[n, at_, :] - top)
            E[n, at_, :] = expo
            weighted = expo * PU[n, at_, :]
            return (
                sums[0] + jnp.sum(expo.reshape(STEP // 8, 8, T), axis=0),
                sums[1] + jnp.sum(weighted.reshape(STEP // 8, 8, T), axis=0),
            )

        zero = jnp.zeros((8, T), F32)
        total, weighted = lax.fori_loop(0, NX * K // STEP, rows, (zero, zero))
        total = jnp.sum(total, axis=0, keepdims=True)
        weighted = jnp.sum(weighted, axis=0, keepdims=True)
        ST[q] = jnp.concatenate([top, total, weighted, jnp.zeros((5, T), F32)], axis=0)

    order = [tile(h, c_, yl_) for h in range(2) for c_, yl_ in groups]

    def both(h, c_):
        one, two = ST[tile(h, c_, 0)], ST[tile(h, c_, 1)]
        tops = [one[0:1], two[0:1]]
        return jnp.concatenate([*tops, *tops, one[1:2], two[1:2], one[2:3], two[2:3]], axis=0)

    def stats_core(h):
        SC[h] = both(h, 1 - c)
        send(SC.at[h], SCR.at[h], at(dc=1), S_SC + h)

    def stats_y(h):
        mine = both(h, c)
        recv(SCR.at[h], S_SC + h)
        SY[h, 0] = merge([mine, SCR[h]])
        for d in range(1, NY):
            send(SY.at[h, 0], SY.at[h, d], at(dy=d), S_SY + 4 * h + d)

    def stats_z(h):
        for d in range(1, NY):
            recv(SY.at[h, d], S_SY + 4 * h + d)
        SZ[h, 0] = merge([SY[h, d] for d in range(NY)])
        for d in range(1, NZ):
            send(SZ.at[h, 0], SZ.at[h, d], diag(d), S_SZ + 8 * h + d)

    def stats_last(h):
        for d in range(1, NZ):
            recv(SZ.at[h, d], S_SZ + 8 * h + d)
        FIN[h, c] = merge([SZ[h, d] for d in range(NZ)])
        send(FIN.at[h, c], FIN.at[h, c], at(dc=1), S_SF + h)

    def stats_end(h):
        recv(FIN.at[h, 1 - c], S_SF + h)

    base = ((yl * NZ + z) * NC + c) * 8 + yh

    def hard_rows(d):
        first_code = (base + (x + d) % NX * 2) * K
        ids = first_code + lax.broadcasted_iota(jnp.int32, (K, 8 * T), 0)
        row = jnp.concatenate(
            [HC[g * 2 + b][0:1, h * half:(h + 1) * half] for h in range(2) for g in range(4) for b in range(2)],
            axis=1,
        )
        hit = jnp.where(row == ids, 1.0, 0.0).astype(BF16)
        H[d] = jnp.dot(hit, GR[...], preferred_element_type=F32)

    def latent_grad(n):
        q = order[n]
        pair = FIN[n // 4, q // 2 % 2]
        fin = jnp.where(q % 2 == 0, pair, pltpu.roll(pair, 7, axis=0))
        inverse = 1.0 / fin[4:5]
        factor = jnp.exp(ST[q][0:1] - fin[0:1]) * inverse
        dlog = ((E[n] * factor) * (PU[n] - fin[6:7] * inverse)).astype(BF16)
        D[:, tokens(q)] = dlog
        return jnp.dot(CBT[...], dlog, preferred_element_type=F32).T

    def latent_other(h):
        for k in range(2):
            GCT[h, k] = latent_grad(4 * h + 2 + k)
            send(GCT.at[h, k], GCR.at[h, k], at(dc=1), S_GC + 2 * h + k)

    def latent_own(h):
        for k in (1, 0):
            total = latent_grad(4 * h + k)
            recv(GCR.at[h, k], S_GC + 2 * h + k)
            GYK[h, k] = total + GCR[h, k]
            GYT[h, k] = GYK[h, k].astype(BF16)

            def part_of(b):
                return GYT.at[h, k, pl.ds(pl.multiple_of(b * half, half), half)]

            if k:
                for b in range(2):
                    dev = device(x, b * 2 + 1 - yl, z, c)
                    send(part_of(b), GYR.at[h, y], dev, S_GY + 4 * h + b, S_GY + 4 * h + y)
            else:
                send(part_of(1 - yh), GYR.at[h, y], at(dy=2), S_GY + 4 * h + 2, S_GY + 4 * h + y)

    def rows_of(x_, yh_, first=0):
        return pl.ds(pl.multiple_of(first + (x_ * 2 + yh_) * part, part), part)

    def latent_home(h):
        total = GYK[h, 0, pl.ds(pl.multiple_of(yh * half, half), half), :]
        for d in range(1, NY):
            y_ = (y + d) % NY
            recv(GYR.at[h, y_], S_GY + 4 * h + y_)
            total = total + GYR[h, y_].astype(F32)
        GZT[h] = total.astype(BF16)
        for dx, dh in xh:
            x_ = (x + dx) % NX
            yh_ = (yh + dh) % 2
            src = GZT.at[h, rows_of(x_, yh_)]
            dev = device(x_, yh_ * 2 + yl, zt + 4 * yh, c)
            if dx or dh:
                send(src, GZR.at[h, z], dev, S_GZ + 8 * h + dx * 2 + dh, S_GZ + 8 * h + z)
            else:
                @pl.when(jnp.logical_not(home))
                def _(src=src, dev=dev):
                    send(src, GZR.at[h, z], dev, S_GZ + 8 * h, S_GZ + 8 * h + z)

                @pl.when(home)
                def _():
                    GZR[h, z] = GZT[h, rows_of(x, yh), :]

    def latent_spread(h):
        for zs in range(NZ):
            @pl.when(jnp.logical_not(home & (z == zs)))
            def _(zs=zs):
                recv(GZR.at[h, zs], S_GZ + 8 * h + zs)
        total = GZR[h, 0].astype(F32)
        for zs in range(1, NZ):
            total = total + GZR[h, zs].astype(F32)
        rows = rows_of(x, yh, h * half)
        GA[h] = total
        for dx, dh in xh[1:]:
            send(GA.at[h], olat.at[rows], across(dx, dh), S_AG + 8 * h + dx * 2 + dh)
        local(GA.at[h], olat.at[rows], 5 + h).start()

    def codebook_grad(d):
        return H[d] + jnp.dot(D[codes((x + d) % NX), :], LAT[...], preferred_element_type=F32)

    def codebook_far():
        GXT[2] = codebook_grad(2).astype(BF16)
        send(GXT.at[2, first_half], GXR.at[2, first_half], at(dx=1), S_GX)
        send(GXT.at[2, second_half], GXR.at[2, second_half], at(dx=3), S_GX + 2)

    def codebook_send(d):
        rows = first_half if d == 1 else second_half
        OC[...] = codebook_grad(d)
        recv(GXR.at[2, rows], S_GX + d - 1)
        OC[rows, :] = OC[rows, :] + GXR[2, rows, :].astype(F32)
        GXT[d] = OC[...].astype(BF16)
        send(GXT.at[d], GXR.at[d], at(dx=d), S_GX + d)

    first(0)
    from_z(3)
    from_core(0)
    from_core(1)
    first(1)
    from_y(2)
    from_z(4)
    first(2)
    first(3)
    stats_core(0)
    from_y(3)
    from_y(4)
    first(4)
    stats_y(0)
    first(5)
    for p in range(2, 5):
        from_core(p)
    first(6)
    stats_z(0)
    first(7)
    stats_core(1)
    hard_rows(2)
    stats_y(1)
    hard_rows(1)
    hard_rows(3)
    CBT[...] = CB[...].T
    stats_last(0)
    stats_z(1)
    stats_end(0)
    latent_other(0)
    latent_own(0)
    hard_rows(0)
    stats_last(1)
    stats_end(1)
    latent_other(1)
    latent_home(0)
    latent_own(1)
    codebook_far()
    latent_home(1)
    latent_spread(0)
    codebook_send(1)
    codebook_send(3)
    latent_spread(1)
    total = codebook_grad(0)
    for d in (1, 3):
        recv(GXR.at[d], S_GX + d)
        total = total + GXR[d].astype(F32)
    OC[...] = total
    out = local(OC, ocb, 7)
    out.start()

    for h in range(2):
        for dx, dh in xh[1:]:
            rows = rows_of((x + NX - dx) % NX, (yh + dh) % 2, h * half)
            recv(olat.at[rows], S_AG + 8 * h + dx * 2 + dh)
        local(GA.at[h], olat.at[rows_of(x, yh, h * half)], 5 + h).wait()
    out.wait()

    for n in range(4):
        sent(cb.at[first_half], S_X + n)
    sent(far_refs[0], S_X + 4)
    sent(far_refs[1], S_X + 5)
    for p in range(5):
        for b in range(2):
            @pl.when(away[b])
            def _(p=p, b=b):
                sent(own[p], S_Z + b * 5 + p)

        sent(refs[0][p], S_YA + p)
        sent(refs[1][p], S_YB + p)
        for k in range(4):
            sent(refs[k][p], S_C + 5 * k + p)
    for h in range(2):
        sent(SC.at[h], S_SC + h)
        sent(SC.at[h], S_SF + h)
        for d in range(1, NY):
            sent(SC.at[h], S_SY + 4 * h + d)
        for d in range(1, NZ):
            sent(SC.at[h], S_SZ + 8 * h + d)
        for k in range(2):
            sent(GCT.at[h, k], S_GC + 2 * h + k)
        for n in range(3):
            sent(GYR.at[0, 0], S_GY + 4 * h + n)
        for n in range(1, 8):
            sent(GZR.at[0, 0], S_GZ + 8 * h + n)
            sent(GA.at[h], S_AG + 8 * h + n)

        @pl.when(jnp.logical_not(home))
        def _(h=h):
            sent(GZR.at[0, 0], S_GZ + 8 * h)
    for d in (1, 3):
        sent(GXT.at[2, first_half], S_GX + d - 1)
        sent(GXT.at[d], S_GX + d)


def place(one, two, out_one, out_two, sems):
    copies = []
    for src, dst in ((one, out_one), (two, out_two)):
        for first in range(0, src.shape[0], 128):
            rows = pl.ds(first, 128)
            copies.append(pltpu.make_async_copy(src.at[rows], dst.at[rows], sems.at[len(copies)]))
    for one_copy in copies:
        one_copy.start()
    for one_copy in copies:
        one_copy.wait()


def per_device(latents, grads, codebook, hard_code):
    T, W = latents.shape
    K = codebook.shape[0]
    part = T // 16
    half = T // 2
    vmem = pl.BlockSpec(memory_space=pltpu.VMEM)
    hbm = pl.BlockSpec(memory_space=pl.ANY)
    scratch = [
        ((8 * T, W), BF16),
        ((8 * T, W), BF16),
        ((8, 8, T), jnp.int32),
        ((8, T), jnp.int32),
        ((NX * K, W), BF16),
        ((W, NX * K), BF16),
        ((8, NX * K, T), F32),
        ((8, NX * K, T), F32),
        ((NX * K, 8 * T), BF16),
        ((NX, K, W), F32),
        ((8, 8, T), F32),
        ((2, 8, T), F32),
        ((2, 8, T), F32),
        ((2, NY, 8, T), F32),
        ((2, NZ, 8, T), F32),
        ((2, 2, 8, T), F32),
        ((2, 2, T, W), F32),
        ((2, 2, T, W), F32),
        ((2, 2, T, W), F32),
        ((2, 2, T, W), BF16),
        ((2, 4, half, W), BF16),
        ((2, half, W), BF16),
        ((2, NZ, part, W), BF16),
        ((2, part, W), F32),
        ((NX, K, W), BF16),
        ((NX, K, W), BF16),
        ((K, W), F32),
    ]
    results = pl.pallas_call(
        kernel,
        out_shape=(jax.ShapeDtypeStruct((T, W), F32), jax.ShapeDtypeStruct((K, W), F32)),
        in_specs=[hbm, hbm, hbm, vmem],
        out_specs=(hbm, hbm),
        scratch_shapes=[pltpu.VMEM(s, t) for s, t in scratch]
        + [pltpu.SemaphoreType.DMA((n,)) for n in (S_ALL, S_ALL, 8)],
        compiler_params=pltpu.CompilerParams(
            collective_id=0, has_side_effects=True, vmem_limit_bytes=62 * 2**20
        ),
    )(latents, grads, codebook, hard_code)
    return pl.pallas_call(
        place,
        out_shape=(jax.ShapeDtypeStruct((T, W), F32), jax.ShapeDtypeStruct((K, W), F32)),
        in_specs=[hbm, hbm],
        out_specs=(hbm, hbm),
        scratch_shapes=[pltpu.SemaphoreType.DMA((6,))],
    )(*results)


def solution(mesh):
    return jax.shard_map(
        per_device,
        mesh=mesh,
        in_specs=(P("dp", None), P("dp", None), P(("dp", "code"), None), P("dp")),
        out_specs=(P("dp", None), P(("dp", "code"), None)),
        check_vma=False,
    )
```
